512 devices in a mesh: blk: 64 (over z, y), obs: 8 (over x, core).
Axes of the slice: x: 4, y: 4, z: 16, core: 2. Of those that a mesh axis runs over, the one named last changes fastest.
Arguments:
- populations: float32 [64, 19, 32, 1024], P('blk', None, 'obs'), may hold values from 0.011111111 to 0.533333333, as said below
- block_faces: int32 [64, 4], P('blk'), may hold values from 0 to 63, as said below
- block_edges: int32 [64, 4], P('blk'), may hold values from 0 to 63, as said below
- probe_cell: int32 [65536], P(('blk', 'obs')), may hold values from 0 to 4095
- history: bfloat16 [65536, 512], P(('blk', 'obs')), may hold values from -6 to 6
- panel_count: int32 [512], P(('blk', 'obs')), may hold values from 0 to 128, as said below
- panel_owner: int32 [65536], P(('blk', 'obs')), may hold values from 0 to 4095, as said below
- panel_pos: bfloat16 [3, 32768], P(None, ('blk', 'obs')), may hold values from -1 to 1
- panel_normal: bfloat16 [3, 32768], P(None, ('blk', 'obs')), may hold values from -0.15625 to 0.15625
- observers: float32 [3, 1024], P(None, 'obs'), may hold values from -8 to 8, as said below
Outputs:
- populations_out: float32 [64, 19, 32, 1024], P('blk', None, 'obs')
- spectrum: float32 [8, 128, 128], P('obs', 'blk')
The draws below stay inside these ranges and needn't reach their ends.
Inputs may be any that keep to these rules, and one draw needn't show every extreme that they name: `populations`: every population is positive. The blocks form a lattice of 16 by 4 blocks along y and z, periodic in both, one block deep in x; block_faces[b] names the blocks beside b at -y, +y, -z, +z. block_edges[b] names the blocks at (-y,-z), (-y,+z), (+y,-z), (+y,+z) of b: the y neighbour's z neighbour, which is the z neighbour's y neighbour. The eight face and edge neighbours of a block are distinct and differ from it. The live slots of a device are its first panel_count slots. The counts of the devices at one obs index sum to 4096. `panel_owner`: in a live slot of the device at blk index b and obs index o the value is q * 64 + j: slot j of the owner at blk index q and the same obs index. Every owner slot receives exactly one live panel. A device sends at most 2 live panels to one owner, and its live panels go to the owners in numbers that differ by at most one. Dead slots hold arbitrary values of the range. `observers`: every observer lies at a distance of 4 to 8 from the anchor (0, 0, 0).
All inputs are finite; a program needn't handle non-finite values.
Results may differ from the reference program's by a relative error of at most 0.0032.
The reference program's roundings to bfloat16 on the way (of `recent`, `owned`, `transform_table` and `spectra`) count: a program that leaves them out, or rounds other values in their place, can miss the bound.
Values may be sent and summed in bfloat16 or wider, within the bound.
No kernel may reach another device: no remote copies, remote signals or barrier semaphores. Data moves between devices by JAX's collectives and lax.ppermute only.
A program may use at most 128 MiB of HBM per device.

```python
import math
import jax
import jax.numpy as jnp
from jax import lax

BS = 32
STEPS = 4
LZ = 4
SAMPLES = 256
BINS = 64
OBSERVERS = 1024
P_OWN = 64
BLOCKS = 64
LY = 16
SLAB = 4
S_DEV = 128
PANELS = 32768
SLOTS = 65536
N_OBS = 8


velocity_list = [(0, 0, 0), (1, 0, 0), (-1, 0, 0), (0, 1, 0), (0, -1, 0), (0, 0, 1), (0, 0, -1), (1, 1, 0), (-1, -1, 0), (1, -1, 0), (-1, 1, 0), (1, 0, 1), (-1, 0, -1), (1, 0, -1), (-1, 0, 1), (0, 1, 1), (0, -1, -1), (0, 1, -1), (0, -1, 1)]


weight_list = [1.0 / 3.0] + [1.0 / 18.0] * 6 + [1.0 / 36.0] * 12


def draw_populations(key, part):
    shape = (BLOCKS, 19, BS, BS * BS)
    weights = jnp.array(weight_list, jnp.float32)[None, :, None, None]
    noise = jnp.clip(jax.random.normal(key, shape, jnp.float32), -6.0, 6.0)
    return weights * (1.0 + 0.1 * noise)


def lattice(key):
    order = jax.random.permutation(jax.random.fold_in(key, 11), BLOCKS).astype(jnp.int32)
    placed = jnp.argsort(order).astype(jnp.int32)
    row_index = placed // LZ
    column_index = placed % LZ

    def beside(move_y, move_z):
        return order[(row_index + move_y) % LY * LZ + (column_index + move_z) % LZ]
    faces_list = jnp.stack([beside(-1, 0), beside(1, 0), beside(0, -1), beside(0, 1)], axis=1)
    edges_list = jnp.stack([beside(-1, -1), beside(-1, 1), beside(1, -1), beside(1, 1)], axis=1)
    return (faces_list.astype(jnp.int32), edges_list.astype(jnp.int32))


def draw_block_faces(key, part):
    return lattice(key)[0]


def draw_block_edges(key, part):
    return lattice(key)[1]


def ownership(key):
    groups = SLOTS // (S_DEV * BLOCKS)

    def one_group(subkey):
        shuffle = jax.random.permutation(jax.random.fold_in(subkey, 1), BLOCKS).astype(jnp.int32)
        halves = BLOCKS // 2
        surplus = jax.random.randint(jax.random.fold_in(subkey, 2), (halves,), 0, P_OWN + 1).astype(jnp.int32)
        surplus = surplus.at[0].set(P_OWN)
        paired = jnp.concatenate([P_OWN + surplus, P_OWN - surplus]).astype(jnp.int32)
        counts = jnp.zeros((BLOCKS,), jnp.int32).at[shuffle].set(paired)
        starts = jnp.cumsum(counts) - counts
        slot_index = jnp.arange(S_DEV, dtype=jnp.int32)
        global_rank = starts[:, None] + slot_index[None, :]
        alive_slot = slot_index[None, :] < counts[:, None]
        relabel = jax.random.permutation(jax.random.fold_in(subkey, 3), BLOCKS).astype(jnp.int32)
        spots = jax.random.permutation(jax.random.fold_in(subkey, 4), P_OWN).astype(jnp.int32)
        target = relabel[global_rank % BLOCKS]
        position = spots[jnp.minimum(global_rank // BLOCKS, P_OWN - 1)]
        filler = jax.random.randint(jax.random.fold_in(subkey, 5), (BLOCKS, S_DEV), 0, BLOCKS * P_OWN).astype(jnp.int32)
        owners = jnp.where(alive_slot, target * P_OWN + position, filler).astype(jnp.int32)
        return (counts, owners)
    counts, owners = jax.vmap(one_group)(jax.random.split(jax.random.fold_in(key, 23), groups))
    counts = counts.transpose(1, 0).reshape(-1).astype(jnp.int32)
    owners = owners.transpose(1, 0, 2).reshape(-1).astype(jnp.int32)
    return (counts, owners)


def draw_panel_count(key, part):
    return ownership(key)[0]


def draw_panel_owner(key, part):
    return ownership(key)[1]


def draw_observers(key, part):
    first_key, second_key, third_key = jax.random.split(key, 3)
    radius = jax.random.uniform(first_key, (OBSERVERS,), jnp.float32, 4.0, 8.0)
    height = jax.random.uniform(second_key, (OBSERVERS,), jnp.float32, -1.0, 1.0)
    heading = jax.random.uniform(third_key, (OBSERVERS,), jnp.float32, 0.0, 2.0 * math.pi)
    spread = jnp.sqrt(jnp.maximum(1.0 - height * height, 0.0))
    return jnp.stack([radius * spread * jnp.cos(heading), radius * spread * jnp.sin(heading), radius * height])


def with_ends(drawn, own_key, least, largest):
    spot = [jax.random.randint(jax.random.fold_in(own_key, axis), (), 0, length) for axis, length in enumerate(drawn.shape)]
    longest = drawn.shape.index(max(drawn.shape))
    neighbour = spot[:longest] + [(spot[longest] + 1) % drawn.shape[longest]] + spot[longest + 1:]
    return drawn.at[tuple(spot)].set(least).at[tuple(neighbour)].set(largest)


def block_levels(key, dims, cuts, low, largest):
    level = 1.0
    for dim, blocks in cuts:
        heights = jax.random.uniform(jax.random.fold_in(jax.random.fold_in(key, 6), dim), (blocks,), jnp.float32, low / len(cuts), largest / len(cuts))
        level = level * jnp.repeat(jnp.exp(heights), dims[dim] // blocks).reshape((-1,) + (1,) * (len(dims) - 1 - dim))
    return level


def normal_values(own_key, dims, deviation, most, pieces=(), kind=jnp.bfloat16):
    result = jax.random.normal(own_key, dims, jnp.float32) * deviation
    if len(pieces) > 0:
        result = block_levels(own_key, dims, pieces, -0.22, 0.18) * result
    return jnp.clip(result, min=-most, max=most).astype(kind)


def setup_inputs(seed: int = 0) -> dict:
    splits = jax.random.split(jax.random.key(seed), 11)
    return {
        "populations": draw_populations(jax.random.fold_in(splits[10], 71), 0),
        "block_faces": draw_block_faces(jax.random.fold_in(splits[10], 71), 0),
        "block_edges": draw_block_edges(jax.random.fold_in(splits[10], 71), 0),
        "probe_cell": with_ends(jax.random.randint(splits[3], (SLOTS,), 0, SLAB * BS * BS), jax.random.fold_in(splits[3], 1), 0, (SLAB * BS * BS) - 1).astype(jnp.int32),
        "history": normal_values(splits[4], (SLOTS, 2 * SAMPLES), 1.0, 6.0, ((0, 512),)),
        "panel_count": draw_panel_count(jax.random.fold_in(splits[10], 71), 0),
        "panel_owner": draw_panel_owner(jax.random.fold_in(splits[10], 71), 0),
        "panel_pos": jnp.clip(jax.random.uniform(splits[7], (3, PANELS), jnp.float32, -1.0, 1.0) * block_levels(splits[7], (3, PANELS), ((1, 512),), -0.4, 0.0), -1.0, 1.0).astype(jnp.bfloat16),
        "panel_normal": normal_values(splits[8], (3, PANELS), (2.0 / PANELS ** 0.5), 0.15625, ((1, 512),)),
        "observers": draw_observers(jax.random.fold_in(splits[10], 71), 0),
    }


velocity_list = [(0, 0, 0), (1, 0, 0), (-1, 0, 0), (0, 1, 0), (0, -1, 0), (0, 0, 1), (0, 0, -1), (1, 1, 0), (-1, -1, 0), (1, -1, 0), (-1, 1, 0), (1, 0, 1), (-1, 0, -1), (1, 0, -1), (-1, 0, 1), (0, 1, 1), (0, -1, -1), (0, 1, -1), (0, -1, 1)]
weight_list = [1.0 / 3.0] + [1.0 / 18.0] * 6 + [1.0 / 36.0] * 12
relax_rate = 1.6
pressure_gain = 60.0
sound_speed = 0.5

def component(axis_number, extra):
    values = jnp.array([velocity[axis_number] for velocity in velocity_list], jnp.float32)
    return values.reshape((19,) + extra)

def collide(field):
    extra = (1,) * (field.ndim - 1)
    along_x = component(0, extra)
    along_y = component(1, extra)
    along_z = component(2, extra)
    weights = jnp.array(weight_list, jnp.float32).reshape((19,) + extra)
    density = lax.optimization_barrier(jnp.sum(field, axis=0))
    speed_x = lax.optimization_barrier(jnp.sum(along_x * field, axis=0)) / density
    speed_y = lax.optimization_barrier(jnp.sum(along_y * field, axis=0)) / density
    speed_z = lax.optimization_barrier(jnp.sum(along_z * field, axis=0)) / density
    projected = along_x * speed_x + along_y * speed_y + along_z * speed_z
    squared = speed_x * speed_x + speed_y * speed_y + speed_z * speed_z
    equilibrium = weights * density * (1.0 + 3.0 * projected + 4.5 * projected * projected - 1.5 * squared)
    return field + relax_rate * (equilibrium - field)

def propagate(padded):
    width_x = padded.shape[1] - 2
    width_y = padded.shape[2] - 2
    width_z = padded.shape[3] - 2
    parts = []
    for number, velocity in enumerate(velocity_list):
        shift_x, shift_y, shift_z = velocity
        parts.append(padded[number, 1 - shift_x:1 - shift_x + width_x, 1 - shift_y:1 - shift_y + width_y, 1 - shift_z:1 - shift_z + width_z])
    return jnp.stack(parts)

def pad_blocks(collided, block_faces, block_edges):
    top_index = BS - 1
    wrapped = jnp.concatenate([collided[:, :, -1:], collided, collided[:, :, :1]], axis=2)
    below_rows = wrapped[:, :, :, top_index:BS, :][block_faces[:, 0]]
    above_rows = wrapped[:, :, :, 0:1, :][block_faces[:, 1]]
    tall_block = jnp.concatenate([below_rows, wrapped, above_rows], axis=3)
    near_core = wrapped[:, :, :, :, top_index:BS][block_faces[:, 2]]
    far_core = wrapped[:, :, :, :, 0:1][block_faces[:, 3]]
    corner_ll = wrapped[:, :, :, top_index:BS, top_index:BS][block_edges[:, 0]]
    corner_lh = wrapped[:, :, :, top_index:BS, 0:1][block_edges[:, 1]]
    corner_hl = wrapped[:, :, :, 0:1, top_index:BS][block_edges[:, 2]]
    corner_hh = wrapped[:, :, :, 0:1, 0:1][block_edges[:, 3]]
    near_plane = jnp.concatenate([corner_ll, near_core, corner_hl], axis=3)
    far_plane = jnp.concatenate([corner_lh, far_core, corner_hh], axis=3)
    return jnp.concatenate([near_plane, tall_block, far_plane], axis=4)

def transform_table():
    moments = jnp.arange(SAMPLES, dtype=jnp.int32)[:, None]
    harmonics = jnp.arange(BINS, dtype=jnp.int32)[None, :] + 1
    turns = moments * harmonics % SAMPLES
    phases = turns.astype(jnp.float32) * (2.0 * math.pi / SAMPLES)
    return jnp.concatenate([jnp.cos(phases), -jnp.sin(phases)], axis=1).astype(jnp.bfloat16)

def radiate(spectra, place, normal, listen):
    values = spectra.astype(jnp.float32)
    press_real = values[0:BINS].T
    press_imag = values[BINS:2 * BINS].T
    rate_real = values[2 * BINS:3 * BINS].T
    rate_imag = values[3 * BINS:4 * BINS].T
    offsets = listen[:, None, :] - place.astype(jnp.float32)[:, :, None]
    distance_sq = lax.optimization_barrier(jnp.sum(offsets * offsets, axis=0))
    distance = jnp.sqrt(distance_sq)
    facing = lax.optimization_barrier(jnp.sum(normal.astype(jnp.float32)[:, :, None] * offsets, axis=0))
    far_term = facing / (4.0 * math.pi * sound_speed * distance_sq)
    near_term = facing / (4.0 * math.pi * distance_sq * distance)
    angular = (jnp.arange(BINS, dtype=jnp.float32) + 1.0) * (2.0 * math.pi / SAMPLES)
    phases = angular[None, :, None] * (distance / sound_speed)[:, None, :]
    cosine = jnp.cos(phases)
    sine_part = jnp.sin(phases)
    weight_real = far_term[:, None, :] * rate_real[:, :, None] + near_term[:, None, :] * press_real[:, :, None]
    weight_imag = far_term[:, None, :] * rate_imag[:, :, None] + near_term[:, None, :] * press_imag[:, :, None]
    real_part = lax.optimization_barrier(jnp.sum(weight_real * cosine + weight_imag * sine_part, axis=0))
    imag_part = lax.optimization_barrier(jnp.sum(weight_imag * cosine - weight_real * sine_part, axis=0))
    return jnp.concatenate([real_part, imag_part], axis=0).T

def reference(populations, block_faces, block_edges, probe_cell, history, panel_count, panel_owner, panel_pos, panel_normal, observers):
    field = populations.reshape(BLOCKS, 19, BS, BS, BS)
    device_of = jnp.arange(SLOTS, dtype=jnp.int32) // S_DEV
    block_of = device_of // N_OBS
    group_of = device_of % N_OBS
    depth = group_of * (BS // N_OBS) + probe_cell // (BS * BS)
    across = probe_cell % (BS * BS)
    readings = []
    for turn_index in range(STEPS):
        collided = jax.vmap(collide)(field)
        field = jax.vmap(propagate)(pad_blocks(collided, block_faces, block_edges))
        density = lax.optimization_barrier(jnp.sum(field, axis=1)).reshape(BLOCKS, BS, BS * BS)
        readings.append(density[block_of, depth, across])
    gained = pressure_gain * (jnp.stack(readings, axis=1) - 1.0)
    previous = jnp.concatenate([history[:, SAMPLES - 1:SAMPLES].astype(jnp.float32), gained[:, :-1]], axis=1)
    rate_values = gained - previous
    recent = jnp.concatenate([history[:, STEPS:SAMPLES], gained.astype(jnp.bfloat16), history[:, SAMPLES + STEPS:], rate_values.astype(jnp.bfloat16)], axis=1)
    slot_local = jnp.arange(SLOTS, dtype=jnp.int32) % S_DEV
    alive_slot = slot_local < panel_count[device_of]
    target = (panel_owner // P_OWN * N_OBS + group_of) * P_OWN + panel_owner % P_OWN
    target = jnp.where(alive_slot, target, PANELS).astype(jnp.int32)
    owned = jnp.zeros((PANELS, 2 * SAMPLES), jnp.bfloat16).at[target].set(recent, mode='drop')
    spectra = jnp.dot(owned.reshape(PANELS * 2, SAMPLES), transform_table(), preferred_element_type=jnp.float32).astype(jnp.bfloat16).reshape(PANELS, 4 * BINS)
    block_size = 256 if PANELS % 256 == 0 else PANELS
    counted = PANELS // block_size
    spectra_blocks = spectra.T.reshape(4 * BINS, counted, block_size).transpose(1, 0, 2)
    place_blocks = panel_pos.reshape(3, counted, block_size).transpose(1, 0, 2)
    normal_blocks = panel_normal.reshape(3, counted, block_size).transpose(1, 0, 2)

    def accumulate(total, inputs):
        return (total + radiate(inputs[0], inputs[1], inputs[2], observers), None)
    total, unused_out = lax.scan(accumulate, jnp.zeros((OBSERVERS, 2 * BINS), jnp.float32), (spectra_blocks, place_blocks, normal_blocks))
    return (field.reshape(BLOCKS, 19, BS, BS * BS), total.reshape(N_OBS, OBSERVERS // N_OBS, 2 * BINS))
```

```python
import functools
import math

import jax
import jax.numpy as jnp
import numpy as np
from jax import lax
from jax.experimental import pallas as pl
from jax.experimental.pallas import tpu as pltpu
from jax.sharding import PartitionSpec as P

BS = 32
STEPS = 4
SAMPLES = 256
BINS = 64
P_OWN = 64
SLAB = 4
CELLS = BS * BS
HALO = 4
PITCH = BS + 2 * HALO
LANES = 1664

VEL = [
    (0, 0, 0),
    (1, 0, 0),
    (-1, 0, 0),
    (0, 1, 0),
    (0, -1, 0),
    (0, 0, 1),
    (0, 0, -1),
    (1, 1, 0),
    (-1, -1, 0),
    (1, -1, 0),
    (-1, 1, 0),
    (1, 0, 1),
    (-1, 0, -1),
    (1, 0, -1),
    (-1, 0, 1),
    (0, 1, 1),
    (0, -1, -1),
    (0, 1, -1),
    (0, -1, 1),
]
WEIGHT = [1.0 / 3.0] + [1.0 / 18.0] * 6 + [1.0 / 36.0] * 12
PAIRS = [(1, 2), (3, 4), (5, 6), (7, 8), (9, 10), (11, 12), (13, 14), (15, 16), (17, 18)]
RELAX = 1.6
GAIN = 60.0
SOUND = 0.5
f32 = jnp.float32
bf16 = jnp.bfloat16

FACE_AXIS = [(1, -1), (1, 1), (2, -1), (2, 1)]


def classes(face):
    axis, sign = FACE_AXIS[face]
    inward = [i for i, v in enumerate(VEL) if v[axis] == sign]
    along = [i for i, v in enumerate(VEL) if v[axis] == 0]
    outward = [i for i, v in enumerate(VEL) if v[axis] == -sign]
    return inward, along, outward


def ext(y, z):
    return (y + HALO) * PITCH + z + HALO


def pick_table():
    out = np.zeros((CELLS, 640), np.float32)
    for d in range(HALO):
        for k in range(BS):
            out[d * BS + k, d * BS + k] = 1
            out[(BS - 1 - d) * BS + k, 128 + d * BS + k] = 1
            out[k * BS + d, 256 + d * BS + k] = 1
            out[k * BS + BS - 1 - d, 384 + d * BS + k] = 1
    for e in range(4):
        for dy in range(HALO):
            for dz in range(HALO):
                y = dy if e < 2 else BS - 1 - dy
                z = dz if e % 2 == 0 else BS - 1 - dz
                lane = e * 16 + dy * HALO + dz
                out[y * BS + z, 512 + lane] = 1
                out[y * BS + z, 512 + 64 + lane] = 1
    return out


def own_table():
    out = np.zeros((CELLS, LANES), np.float32)
    for y in range(BS):
        for z in range(BS):
            out[y * BS + z, ext(y, z)] = 1
    return out


def halo_table():
    out = np.zeros((640, LANES), np.float32)
    for d in range(HALO):
        for k in range(BS):
            out[d * BS + k, ext(BS + d, k)] = 1
            out[128 + d * BS + k, ext(-1 - d, k)] = 1
            out[256 + d * BS + k, ext(k, BS + d)] = 1
            out[384 + d * BS + k, ext(k, -1 - d)] = 1
    for e in range(4):
        for dy in range(HALO):
            for dz in range(HALO):
                y = BS + dy if e < 2 else -1 - dy
                z = BS + dz if e % 2 == 0 else -1 - dz
                lane = e * 16 + dy * HALO + dz
                out[512 + lane, ext(y, z)] = 1
                out[512 + 64 + lane, ext(y, z)] = 1
    return out


def tiles_of(total, step):
    return [(a, min(a + step, total)) for a in range(0, total, step)]


def band(table, lo, hi):
    rows = np.nonzero(table[:, lo:hi].any(axis=1))[0]
    if rows.size == 0:
        return 0, 128
    return int(rows[0]) // 128 * 128, -(-(int(rows[-1]) + 1) // 128) * 128


def transform_table():
    moments = np.arange(SAMPLES)[:, None]
    harmonics = np.arange(BINS)[None, :] + 1
    turns = moments * harmonics % SAMPLES
    phases = turns.astype(np.float32) * np.float32(2.0 * math.pi / SAMPLES)
    table = np.concatenate([np.cos(phases), -np.sin(phases)], axis=1).astype(np.float32)
    return table.astype(jnp.bfloat16)


def collide(fs):
    rho = fs[0]
    for f in fs[1:]:
        rho = rho + f
    speed = []
    for axis in range(3):
        up = [f for f, v in zip(fs, VEL) if v[axis] == 1]
        down = [f for f, v in zip(fs, VEL) if v[axis] == -1]
        speed.append(sum(up[1:], up[0]) - sum(down[1:], down[0]))
    inverse = 1.0 / rho
    speed = [s * inverse for s in speed]
    squared = speed[0] * speed[0] + speed[1] * speed[1] + speed[2] * speed[2]
    base = 1.0 - 1.5 * squared
    out = [None] * 19
    out[0] = (RELAX * WEIGHT[0]) * rho * base + (1.0 - RELAX) * fs[0]
    axis_scale = (RELAX / 18.0) * rho
    diagonal_scale = (RELAX / 36.0) * rho
    for a, b in PAIRS:
        along = None
        for axis in range(3):
            if VEL[a][axis] != 0:
                term = speed[axis]
                if along is None:
                    along = term if VEL[a][axis] == 1 else -term
                else:
                    along = along + term if VEL[a][axis] == 1 else along - term
        scale = axis_scale if a < 7 else diagonal_scale
        even = scale * (base + 4.5 * (along * along))
        odd = scale * (3.0 * along)
        out[a] = even + odd + (1.0 - RELAX) * fs[a]
        out[b] = even - odd + (1.0 - RELAX) * fs[b]
    return out


def pack_kernel(faces, edges, f_ref, pos_ref, nor_ref, pick_ref, c_ref, cb_ref, msg_ref, strip, packed, slots):
    for lo, hi in tiles_of(CELLS, 256):
        fs = [f_ref[0, i, :, lo:hi] for i in range(19)]
        for i, c in enumerate(collide(fs)):
            c_ref[4 * i : 4 * i + 4, lo:hi] = c - WEIGHT[i]
    c_ref[76:80, :] = jnp.zeros((4, CELLS), f32)
    rounded = c_ref[...].astype(bf16)
    cb_ref[...] = rounded
    strip[...] = jnp.dot(rounded, pick_ref[...], preferred_element_type=f32)
    lane4 = lax.broadcasted_iota(jnp.int32, (4, 128), 1)
    for face in range(4):
        inward, along, outward = classes(face)

        def rows(i):
            return strip[4 * i : 4 * i + 4, face * 128 : face * 128 + 128]

        groups = [rows(i) for i in inward] + [rows(i) for i in along]
        last = rows(outward[4])
        groups[5] = jnp.where(lane4 < 96, groups[5], pltpu.roll(last, 96, 1))
        groups[6] = jnp.where(lane4 < 96, groups[6], pltpu.roll(last, 64, 1))
        for a, b in ((0, 1), (2, 3)):
            shifted = pltpu.roll(rows(outward[b]), 64, 1)
            groups.append(jnp.where(lane4 < 64, rows(outward[a]), shifted))
        for g, value in enumerate(groups):
            packed[face * 64 + 4 * g : face * 64 + 4 * g + 4, :] = value
    lane16 = lax.broadcasted_iota(jnp.int32, (16, 128), 1)
    packed[256:320, :] = strip[0:64, 512:640]
    packed[256:272, :] = jnp.where(lane16 < 64, strip[0:16, 512:640], strip[64:80, 512:640])
    for message in range(8):
        source = min(message, 4) * 64
        for r in range(8):
            slots[message * 8 : message * 8 + 8, 128 * r : 128 * r + 128] = packed[
                source + 8 * r : source + 8 * r + 8, :
            ]
    pos = pos_ref[...].astype(f32)
    nor = nor_ref[...].astype(f32)
    pairs = [(pos[0:1], pos[1:2]), (pos[2:3], nor[0:1]), (nor[1:2], nor[2:3])]
    for r, (a, b) in enumerate(pairs):
        row = jnp.concatenate([a, b], axis=1)
        slots[:, 1024 + 128 * r : 1152 + 128 * r] = jnp.broadcast_to(row, (64, 128))
    source_of = [faces[0, 1], faces[0, 0], faces[0, 3], faces[0, 2]]
    source_of += [edges[0, 3], edges[0, 2], edges[0, 1], edges[0, 0]]
    kind = lax.broadcasted_iota(jnp.int32, (64, 128), 0) // 8
    index = jnp.zeros((64, 128), jnp.int32)
    for message in range(8):
        index = jnp.where(kind == message, source_of[message], index)
    slots[:, 1408:1536] = index.astype(f32)
    msg_ref[...] = slots[...].astype(bf16)


def forward_kernel(in_ref, out_ref):
    wanted = in_ref[:, 1408:1472].astype(f32).astype(jnp.int32)
    onehot = wanted == lax.broadcasted_iota(jnp.int32, (64, 64), 1)
    picked = jnp.dot(
        onehot.astype(f32).astype(bf16), in_ref[:, 0:1024], preferred_element_type=f32
    )
    out_ref[...] = picked.astype(bf16)


OWN_ROW, HIGH_ROW = 2, 6


def place_slab(ref, i, slab, value, lanes):
    if slab == 0:
        ref[16 * i + OWN_ROW : 16 * i + OWN_ROW + 4, lanes] = value
    elif slab == 1:
        ref[16 * i + HIGH_ROW : 16 * i + HIGH_ROW + 4, lanes] = value
    else:
        ref[16 * i + 14 : 16 * i + 16, lanes] = value[0:2]
        ref[16 * i : 16 * i + 2, lanes] = value[2:4]


def early_kernel(
    bands, count, c_ref, low_ref, high_ref, geo_ref, owner_ref, hist_ref, table_ref, last_ref,
    *rest,
):
    own_refs, (state, spec, prev, geo, rows) = rest[: len(bands)], rest[len(bands) :]
    low = low_ref[...].astype(f32)
    high = high_ref[...].astype(f32)
    for i in range(19):
        rows[16 * i + 10 : 16 * i + 14, :] = jnp.zeros((4, CELLS), f32)
        place_slab(rows, i, 0, c_ref[4 * i : 4 * i + 4, :], slice(None))
        place_slab(rows, i, -1, low[4 * i : 4 * i + 4], slice(None))
        place_slab(rows, i, 1, high[4 * i : 4 * i + 4], slice(None))
    for (lo, hi, a, b), own_ref in zip(bands, own_refs):
        part = rows[:, a:b]
        coarse = part.astype(bf16)
        fine = (part - coarse.astype(f32)).astype(bf16)
        placed = jnp.dot(coarse, own_ref[...], preferred_element_type=f32)
        placed = placed + jnp.dot(fine, own_ref[...], preferred_element_type=f32)
        state[:, lo:hi] = placed
    nt = (((1,), (1,)), ((), ()))
    spec[0:128, :] = lax.dot_general(table_ref[...], hist_ref[:, 0:256], nt, preferred_element_type=f32)
    spec[128:256, :] = lax.dot_general(table_ref[...], hist_ref[:, 256:512], nt, preferred_element_type=f32)
    prev[...] = lax.dot_general(last_ref[...], hist_ref[:, 0:256], nt, preferred_element_type=f32)
    owner = owner_ref[...]
    step = lax.broadcasted_iota(jnp.int32, (64, 128), 0)
    which = (step == owner // P_OWN).astype(f32).astype(bf16)
    place = (step == owner % P_OWN).astype(f32)
    turned = (((0,), (0,)), ((), ()))
    picked = lax.dot_general(geo_ref[:, 1024:1408], which, turned, preferred_element_type=f32)
    geo[...] = jnp.zeros((16, 128), f32)
    for c in range(6):
        geo[c : c + 1, :] = jnp.sum(picked[64 * c : 64 * c + 64] * place, axis=0, keepdims=True)
    geo[6:7, :] = jnp.full((1, 128), count[0], jnp.int32).astype(f32)


def flow_kernel(
    halo_bands, count, state_ref, own_ref, low_ref, high_ref, cell_ref, spec_ref, prev_ref, geo_ref, late_ref,
    *rest,
):
    halo_refs = rest[: len(halo_bands)]
    out_ref, field_ref, packed, halo, here, there, seen = rest[len(halo_bands) :]
    lane4 = lax.broadcasted_iota(jnp.int32, (4, 128), 1)
    lane64 = lax.broadcasted_iota(jnp.int32, (64, 128), 1)
    for i in range(19):
        halo[16 * i + 10 : 16 * i + 14, :] = jnp.zeros((4, 640), f32)
    for slab, ref in ((0, own_ref), (-1, low_ref), (1, high_ref)):
        for message in range(8):
            value = ref[:, 0:1024].astype(f32)[message * 8 : message * 8 + 8]
            for r in range(8):
                packed[message * 64 + 8 * r : message * 64 + 8 * r + 8, :] = value[:, 128 * r : 128 * r + 128]
        for face in range(4):
            inward, along, outward = classes(face)
            lanes = slice(face * 128, face * 128 + 128)

            def group(g):
                return packed[face * 64 + 4 * g : face * 64 + 4 * g + 4, :]

            for g, i in enumerate(inward + along):
                place_slab(halo, i, slab, group(g), lanes)
            for g, (a, b) in ((14, (0, 1)), (15, (2, 3))):
                place_slab(halo, outward[a], slab, group(g), lanes)
                place_slab(halo, outward[b], slab, pltpu.roll(group(g), 64, 1), lanes)
            last = jnp.where(lane4 < 32, pltpu.roll(group(5), 32, 1), pltpu.roll(group(6), 64, 1))
            place_slab(halo, outward[4], slab, last, lanes)
        corner = packed[256:320, :]
        for e in range(1, 4):
            corner = jnp.where((lane64 % 64) // 16 == e, packed[256 + 64 * e : 320 + 64 * e, :], corner)
        packed[256:320, :] = corner
        for i in range(19):
            rows = packed[256 + 4 * (i % 16) : 260 + 4 * (i % 16), :]
            rows = jnp.where((lane4 < 64) == (i < 16), rows, 0.0)
            place_slab(halo, i, slab, rows, slice(512, 640))
    for (lo, hi, a, b), halo_ref in zip(halo_bands, halo_refs):
        added = jnp.dot(halo[:, a:b].astype(bf16), halo_ref[...], preferred_element_type=f32)
        for i in range(19):
            here[i, :, lo:hi] = state_ref[16 * i : 16 * i + 16, lo:hi] + added[16 * i : 16 * i + 16] + WEIGHT[i]

    lane = lax.broadcasted_iota(jnp.int32, (1, LANES), 1)
    y, z = lane // PITCH - HALO, lane % PITCH - HALO
    inside = (y >= 0) & (y < BS) & (z >= 0) & (z < BS)
    for t in range(STEPS):
        depth_in = 16 if t < 2 else 8
        depth_out = 16 if t < 1 else 8
        for i, (cx, cy, cz) in enumerate(VEL):
            value = here[i, 0:depth_in, :]
            shift = (cy * PITCH + cz) % LANES
            if shift:
                value = pltpu.roll(value, shift, 1)
            if cx:
                value = pltpu.roll(value, cx % depth_in, 0)
            there[i, 0:depth_out, :] = value[0:depth_out]
        total = there[0, 0:8, :]
        for i in range(1, 19):
            total = total + there[i, 0:8, :]
        seen[8 * t : 8 * t + 8, :] = jnp.where(inside, total - 1.0, 0.0)
        if t < STEPS - 1:

            def one(c, _):
                at = pl.ds(pl.multiple_of(c * 128, 128), 128)
                for i, value in enumerate(collide([there[i, 0:depth_out, at] for i in range(19)])):
                    here[i, 0:depth_out, at] = value
                return 0

            lax.fori_loop(0, LANES // 128, one, 0)
    for i in range(19):
        field_ref[8 * i : 8 * i + 8, :] = jnp.where(inside, there[i, 0:8, :], 0.0)

    cell = cell_ref[...]
    across = cell % CELLS
    spot = (across // BS + HALO) * PITCH + across % BS + HALO
    onehot = (lax.broadcasted_iota(jnp.int32, (LANES, 128), 0) == spot).astype(f32).astype(bf16)
    rest_of = seen[...]
    read = jnp.zeros((8 * STEPS, 128), f32)
    for _ in range(3):
        piece = rest_of.astype(bf16)
        read = read + jnp.dot(piece, onehot, preferred_element_type=f32)
        rest_of = rest_of - piece.astype(f32)
    before = prev_ref[0:1, :]
    press, rate = [], []
    for t in range(STEPS):
        value = jnp.zeros((1, 128), f32)
        for x in range(SLAB):
            row = 8 * t + OWN_ROW + x
            value = jnp.where(cell // CELLS == x, read[row : row + 1], value)
        value = GAIN * value
        press.append(value.astype(bf16).astype(f32))
        rate.append((value - before).astype(bf16).astype(f32))
        before = value
    alive = lax.broadcasted_iota(jnp.int32, (1, 128), 1) < count[0]
    for g, late in ((0, press), (1, rate)):
        total = spec_ref[128 * g : 128 * g + 128, :]
        for t in range(STEPS):
            total = total + late_ref[:, t : t + 1] * late[t]
        out_ref[128 * g : 128 * g + 128, :] = jnp.where(alive, total, 0.0).astype(bf16)
    out_ref[256:272, :] = geo_ref[...].astype(bf16)


def field_kernel(bands, field_ref, *rest):
    own_refs, (out_ref,) = rest[: len(bands)], rest[len(bands) :]
    for (lo, hi, a, b), own_ref in zip(bands, own_refs):
        part = field_ref[:, a:b]
        coarse = part.astype(bf16)
        fine = (part - coarse.astype(f32)).astype(bf16)
        value = jnp.dot(coarse, own_ref[...], preferred_element_type=f32)
        value = value + jnp.dot(fine, own_ref[...], preferred_element_type=f32)
        for i in range(19):
            out_ref[0, i, :, lo:hi] = value[8 * i + OWN_ROW : 8 * i + OWN_ROW + 4]


def radiate_kernel(all_ref, listen_ref, out_ref, rows, spots, sums, turned):
    base = jnp.zeros((1, 128), f32)
    lane_f = lax.broadcasted_iota(jnp.int32, (128, 1024), 1).astype(f32)
    slot_f = lax.broadcasted_iota(jnp.int32, (128, 1024), 0).astype(f32)
    for o in range(8):
        live = all_ref[o, 256:272, :].astype(f32)[6:7]
        here = (lane_f - base[:, 0:1] == slot_f) & (slot_f < live[:, 0:1])
        part = jnp.dot(all_ref[o], here.astype(f32).astype(bf16), preferred_element_type=f32)
        if o == 0:
            rows[...] = part
        else:
            rows[...] += part
        base = base + live
    used = jnp.max(base).astype(jnp.int32)
    for axis in range(3):
        row = listen_ref[axis : axis + 1, :]
        spots[axis] = jnp.broadcast_to(row, (128, 128)).T
    sums[...] = jnp.zeros((128, 128, 128), f32)

    def panels(p, _):
        at = pl.ds(pl.multiple_of(p * 128, 128), 128)

        def listeners(m, _):
            ears = pl.ds(pl.multiple_of(m * 16, 16), 16)
            distance_sq = jnp.zeros((16, 128), f32)
            facing = jnp.zeros((16, 128), f32)
            for axis in range(3):
                offset = spots[axis, ears, :] - rows[256 + axis : 257 + axis, at]
                distance_sq = distance_sq + offset * offset
                facing = facing + rows[259 + axis : 260 + axis, at] * offset
            distance = jnp.sqrt(distance_sq)
            far = facing / (4.0 * math.pi * SOUND * distance_sq)
            ratio = SOUND / distance
            angle = (2.0 * math.pi / SAMPLES) * (distance / SOUND)
            cosine = jnp.cos(angle)
            double = cosine + cosine
            c_before, s_before = far, jnp.zeros((16, 128), f32)
            c_now, s_now = far * cosine, far * jnp.sin(angle)
            for k in range(BINS):
                weight_real = rows[128 + k : 129 + k, at] + ratio * rows[k : k + 1, at]
                weight_imag = rows[192 + k : 193 + k, at] + ratio * rows[64 + k : 65 + k, at]
                sums[k, ears, :] += weight_real * c_now + weight_imag * s_now
                sums[BINS + k, ears, :] += weight_imag * c_now - weight_real * s_now
                if k < BINS - 1:
                    c_now, c_before = double * c_now - c_before, c_now
                    s_now, s_before = double * s_now - s_before, s_now
            return 0

        lax.fori_loop(0, 8, listeners, 0)
        return 0

    lax.fori_loop(0, (used + 127) // 128, panels, 0)

    column = lax.broadcasted_iota(jnp.int32, (128, 128), 1)
    turned[...] = jnp.zeros((128, 128), f32)

    def fold(k, _):
        pick = (column == k).astype(f32).astype(bf16)
        value = sums[k]
        coarse = value.astype(bf16)
        fine = (value - coarse.astype(f32)).astype(bf16)
        turned[...] += jnp.dot(coarse, pick, preferred_element_type=f32) + jnp.dot(
            fine, pick, preferred_element_type=f32
        )
        return 0

    lax.fori_loop(0, 128, fold, 0)
    out_ref[...] = turned[...]


def call(kernel, outs, operands, scratch=(), scalars=0, megabytes=32, flops=0):
    smem = pl.BlockSpec(memory_space=pltpu.SMEM)
    vmem = pl.BlockSpec(memory_space=pltpu.VMEM)
    return pl.pallas_call(
        kernel,
        out_shape=tuple(jax.ShapeDtypeStruct(s, d) for s, d in outs),
        in_specs=[smem] * scalars + [vmem] * (len(operands) - scalars),
        out_specs=tuple(vmem for _ in outs),
        scratch_shapes=[pltpu.VMEM(s, f32) for s in scratch],
        compiler_params=pltpu.CompilerParams(vmem_limit_bytes=megabytes * 2**20),
        cost_estimate=pl.CostEstimate(flops=flops, bytes_accessed=2**20, transcendentals=0),
    )(*operands)


def body(
    populations,
    block_faces,
    block_edges,
    probe_cell,
    history,
    panel_count,
    panel_owner,
    panel_pos,
    panel_normal,
    observers,
):
    own = own_table()
    around = halo_table()
    bands = [(lo, hi, *band(own, lo, hi)) for lo, hi in tiles_of(LANES, 256)]
    halo_bands = [(lo, hi, *band(around, lo, hi)) for lo, hi in tiles_of(LANES, 256)]
    back = own.T
    back_bands = [(lo, hi, *band(back, lo, hi)) for lo, hi in tiles_of(CELLS, 256)]

    def cut(table, ranges):
        return [jnp.asarray(table[a:b, lo:hi].astype(jnp.bfloat16)) for lo, hi, a, b in ranges]

    table = transform_table()
    shifted = np.concatenate([np.zeros((STEPS, 128), table.dtype), table[: SAMPLES - STEPS]]).T
    late = np.zeros((128, 128), np.float32)
    late[:, :STEPS] = table[SAMPLES - STEPS :].astype(np.float32).T
    newest = np.zeros((16, SAMPLES), np.float32)
    newest[0, SAMPLES - 1] = 1

    pick = jnp.asarray(pick_table().astype(jnp.bfloat16))
    collided, rounded, message = call(
        pack_kernel,
        [((80, CELLS), f32), ((80, CELLS), bf16), ((64, 1536), bf16)],
        [block_faces, block_edges, populations, panel_pos, panel_normal, pick],
        scratch=[(80, 640), (320, 128), (64, 1536)],
        scalars=2,
    )
    ring = lax.axis_size("obs")
    up = [(i, (i + 1) % ring) for i in range(ring)]
    down = [(i, (i - 1) % ring) for i in range(ring)]

    def beside(value):
        return lax.ppermute(value, "obs", up), lax.ppermute(value, "obs", down)

    low, high = beside(rounded)
    spread = lax.all_to_all(message, "blk", 0, 0, tiled=True)
    (sent,) = call(forward_kernel, [((64, 1024), bf16)], [spread])
    arrived = lax.all_to_all(sent, "blk", 0, 0, tiled=True)
    state, spec, prev, geo = call(
        functools.partial(early_kernel, bands),
        [((304, LANES), f32), ((256, 128), f32), ((16, 128), f32), ((16, 128), f32)],
        [
            panel_count, collided, low, high, spread, panel_owner.reshape(1, 128), history,
            jnp.asarray(shifted), jnp.asarray(newest.astype(jnp.bfloat16)), *cut(own, bands),
        ],
        scratch=[(304, CELLS)],
        scalars=1,
        flops=10**9,
    )
    arrived_low, arrived_high = beside(arrived)
    payload, field = call(
        functools.partial(flow_kernel, halo_bands),
        [((272, 128), bf16), ((152, LANES), f32)],
        [
            panel_count, state, arrived, arrived_low, arrived_high, probe_cell.reshape(1, 128), spec, prev,
            geo, jnp.asarray(late), *cut(around, halo_bands),
        ],
        scratch=[(512, 128), (304, 640), (19, 16, LANES), (19, 16, LANES), (32, LANES)],
        scalars=1,
    )
    (populations_out,) = call(
        functools.partial(field_kernel, back_bands),
        [((1, 19, SLAB, CELLS), f32)],
        [field, *cut(back, back_bands)],
        flops=10**9,
    )
    gathered = lax.all_gather(payload, "obs", axis=0, tiled=False)
    (partial_value,) = call(
        radiate_kernel,
        [((128, 128), f32)],
        [gathered, observers],
        scratch=[(272, 1024), (3, 128, 128), (128, 128, 128), (128, 128)],
        megabytes=48,
    )
    pieces = lax.all_to_all(partial_value.reshape(64, 256), "blk", 0, 0, tiled=True)
    summed = jnp.sum(pieces, axis=0)
    return (populations_out, summed.reshape(1, 2, 2 * BINS))


def solution(mesh):
    placed = (
        P("blk", None, "obs", None),
        P("blk", None),
        P("blk", None),
        P(("blk", "obs")),
        P(("blk", "obs"), None),
        P(("blk", "obs")),
        P(("blk", "obs")),
        P(None, ("blk", "obs")),
        P(None, ("blk", "obs")),
        P(None, "obs"),
    )
    return jax.shard_map(
        body,
        mesh=mesh,
        in_specs=placed,
        out_specs=(P("blk", None, "obs", None), P("obs", "blk", None)),
        check_vma=False,
    )
```

```python
import functools
import math

import jax
import jax.numpy as jnp
import numpy as np
from jax import lax
from jax.experimental import pallas as pl
from jax.experimental.pallas import tpu as pltpu
from jax.sharding import PartitionSpec as P

BS = 32
STEPS = 4
SAMPLES = 256
BINS = 64
P_OWN = 64
SLAB = 4
CELLS = BS * BS
HALO = 4
PITCH = BS + 2 * HALO
LANES = 1664

VEL = [
    (0, 0, 0),
    (1, 0, 0),
    (-1, 0, 0),
    (0, 1, 0),
    (0, -1, 0),
    (0, 0, 1),
    (0, 0, -1),
    (1, 1, 0),
    (-1, -1, 0),
    (1, -1, 0),
    (-1, 1, 0),
    (1, 0, 1),
    (-1, 0, -1),
    (1, 0, -1),
    (-1, 0, 1),
    (0, 1, 1),
    (0, -1, -1),
    (0, 1, -1),
    (0, -1, 1),
]
WEIGHT = [1.0 / 3.0] + [1.0 / 18.0] * 6 + [1.0 / 36.0] * 12
PAIRS = [(1, 2), (3, 4), (5, 6), (7, 8), (9, 10), (11, 12), (13, 14), (15, 16), (17, 18)]
RELAX = 1.6
GAIN = 60.0
SOUND = 0.5
f32 = jnp.float32
bf16 = jnp.bfloat16

FACE_AXIS = [(1, -1), (1, 1), (2, -1), (2, 1)]


def classes(face):
    axis, sign = FACE_AXIS[face]
    inward = [i for i, v in enumerate(VEL) if v[axis] == sign]
    along = [i for i, v in enumerate(VEL) if v[axis] == 0]
    outward = [i for i, v in enumerate(VEL) if v[axis] == -sign]
    return inward, along, outward


def ext(y, z):
    return (y + HALO) * PITCH + z + HALO


def own_table():
    out = np.zeros((CELLS, LANES), np.float32)
    for y in range(BS):
        for z in range(BS):
            out[y * BS + z, ext(y, z)] = 1
    return out


def halo_table():
    out = np.zeros((640, LANES), np.float32)
    for d in range(HALO):
        for k in range(BS):
            out[d * BS + k, ext(BS + d, k)] = 1
            out[128 + d * BS + k, ext(-1 - d, k)] = 1
            out[256 + d * BS + k, ext(k, BS + d)] = 1
            out[384 + d * BS + k, ext(k, -1 - d)] = 1
    for e in range(4):
        for dy in range(HALO):
            for dz in range(HALO):
                y = BS + dy if e < 2 else -1 - dy
                z = BS + dz if e % 2 == 0 else -1 - dz
                lane = e * 16 + dy * HALO + dz
                out[512 + lane, ext(y, z)] = 1
                out[512 + 64 + lane, ext(y, z)] = 1
    return out


def tiles_of(total, step):
    return [(a, min(a + step, total)) for a in range(0, total, step)]


def band(table, lo, hi):
    rows = np.nonzero(table[:, lo:hi].any(axis=1))[0]
    if rows.size == 0:
        return 0, 128
    return int(rows[0]) // 128 * 128, -(-(int(rows[-1]) + 1) // 128) * 128


def transform_table():
    moments = np.arange(SAMPLES)[:, None]
    harmonics = np.arange(BINS)[None, :] + 1
    turns = moments * harmonics % SAMPLES
    phases = turns.astype(np.float32) * np.float32(2.0 * math.pi / SAMPLES)
    table = np.concatenate([np.cos(phases), -np.sin(phases)], axis=1).astype(np.float32)
    return table.astype(jnp.bfloat16)


def collide(fs):
    rho = fs[0]
    for f in fs[1:]:
        rho = rho + f
    speed = []
    for axis in range(3):
        up = [f for f, v in zip(fs, VEL) if v[axis] == 1]
        down = [f for f, v in zip(fs, VEL) if v[axis] == -1]
        speed.append(sum(up[1:], up[0]) - sum(down[1:], down[0]))
    inverse = 1.0 / rho
    speed = [s * inverse for s in speed]
    squared = speed[0] * speed[0] + speed[1] * speed[1] + speed[2] * speed[2]
    base = 1.0 - 1.5 * squared
    out = [None] * 19
    out[0] = (RELAX * WEIGHT[0]) * rho * base + (1.0 - RELAX) * fs[0]
    axis_scale = (RELAX / 18.0) * rho
    diagonal_scale = (RELAX / 36.0) * rho
    for a, b in PAIRS:
        along = None
        for axis in range(3):
            if VEL[a][axis] != 0:
                term = speed[axis]
                if along is None:
                    along = term if VEL[a][axis] == 1 else -term
                else:
                    along = along + term if VEL[a][axis] == 1 else along - term
        scale = axis_scale if a < 7 else diagonal_scale
        even = scale * (base + 4.5 * (along * along))
        odd = scale * (3.0 * along)
        out[a] = even + odd + (1.0 - RELAX) * fs[a]
        out[b] = even - odd + (1.0 - RELAX) * fs[b]
    return out


def strip_rows():
    lane = lax.broadcasted_iota(jnp.int32, (1, 128), 1)
    depth, along = lane // BS, lane % BS
    edge, dy, dz = lane // 16 % 4, lane // HALO % HALO, lane % HALO
    y = jnp.where(edge < 2, dy, BS - 1 - dy)
    z = jnp.where(edge % 2 == 0, dz, BS - 1 - dz)
    return jnp.concatenate([along * BS + depth, along * BS + BS - 1 - depth, y * BS + z], axis=1)


def onehot(condition):
    return condition.astype(f32).astype(bf16)


def pack_kernel(f_ref, shapes_ref, links_ref, c_ref, cb_ref, msg_ref, strip, packed, slots):
    cell = lax.broadcasted_iota(jnp.int32, (CELLS, 384), 0)
    pick = onehot(cell == strip_rows())
    last = lax.broadcasted_iota(jnp.int32, (128, 128), 0)
    lane = lax.broadcasted_iota(jnp.int32, (128, 128), 1)
    turn = onehot(last == (HALO - 1 - lane // BS) * BS + lane % BS)
    for lo, hi in tiles_of(CELLS, 256):
        fs = [f_ref[0, i, :, lo:hi] for i in range(19)]
        for i, c in enumerate(collide(fs)):
            c_ref[4 * i : 4 * i + 4, lo:hi] = c - WEIGHT[i]
    c_ref[76:80, :] = jnp.zeros((4, CELLS), f32)
    rounded = c_ref[...].astype(bf16)
    cb_ref[...] = rounded
    strip[:, 0:128] = rounded[:, 0:128].astype(f32)
    strip[:, 128:256] = jnp.dot(rounded[:, CELLS - 128 :], turn, preferred_element_type=f32)
    strip[:, 256:640] = jnp.dot(rounded, pick, preferred_element_type=f32)
    lane4 = lax.broadcasted_iota(jnp.int32, (4, 128), 1)
    for face in range(4):
        inward, along, outward = classes(face)

        def rows(i):
            return strip[4 * i : 4 * i + 4, face * 128 : face * 128 + 128]

        groups = [rows(i) for i in inward] + [rows(i) for i in along]
        fifth = rows(outward[4])
        groups[5] = jnp.where(lane4 < 96, groups[5], pltpu.roll(fifth, 96, 1))
        groups[6] = jnp.where(lane4 < 96, groups[6], pltpu.roll(fifth, 64, 1))
        for a, b in ((0, 1), (2, 3)):
            shifted = pltpu.roll(rows(outward[b]), 64, 1)
            groups.append(jnp.where(lane4 < 64, rows(outward[a]), shifted))
        for g, value in enumerate(groups):
            packed[face * 64 + 4 * g : face * 64 + 4 * g + 4, :] = value
    lane16 = lax.broadcasted_iota(jnp.int32, (16, 128), 1)
    packed[256:320, :] = strip[0:64, 512:640]
    packed[256:272, :] = jnp.where(lane16 < 64, strip[0:16, 512:640], strip[64:80, 512:640])
    slots[0:32, 0:8, :] = packed[0:256, :].reshape(32, 8, 128)
    for message in range(4, 8):
        slots[message * 8 : message * 8 + 8, 0:8, :] = packed[256:320, :].reshape(8, 8, 128)
    info = shapes_ref[...].astype(f32)
    links = links_ref[...].astype(f32)
    geometry = [jnp.concatenate([info[2 * r : 2 * r + 1], info[2 * r + 1 : 2 * r + 2]], axis=1) for r in range(3)]
    row = lax.broadcasted_iota(jnp.int32, (8, 128), 0)
    for message in range(8):
        line, column = (0, (1, 0, 3, 2)[message]) if message < 4 else (1, 7 - message)
        block = jnp.broadcast_to(links[line : line + 1, column : column + 1], (8, 128))
        for r in range(3):
            block = jnp.where(row == r, geometry[r], block)
        slots[message * 8 : message * 8 + 8, 8:16, :] = jnp.broadcast_to(block[None], (8, 8, 128))
    msg_ref[...] = slots[...].astype(bf16)


def forward_kernel(in_ref, out_ref, geo_ref, rows, moved):
    rows[...] = in_ref[...].astype(f32).reshape(1024, 128)

    def every(r):
        return rows[pl.ds(r, 64, stride=16), :]

    wanted = every(11)[:, 0:64].astype(jnp.int32)
    mine = onehot(wanted == lax.broadcasted_iota(jnp.int32, (64, 64), 1))
    sent = jnp.concatenate([every(r) for r in range(8)], axis=1).astype(bf16)
    picked = jnp.dot(mine, sent, preferred_element_type=f32)
    for r in range(8):
        moved[pl.ds(r, 64, stride=8), :] = picked[:, 128 * r : 128 * r + 128]
    out_ref[...] = moved[...].reshape(64, 8, 128).astype(bf16)
    geo_ref[...] = jnp.concatenate([every(r) for r in range(8, 11)], axis=1).astype(bf16)


OWN_ROW, HIGH_ROW = 2, 6


def place_slab(ref, i, slab, value, lanes):
    if slab == 0:
        ref[16 * i + OWN_ROW : 16 * i + OWN_ROW + 4, lanes] = value
    elif slab == 1:
        ref[16 * i + HIGH_ROW : 16 * i + HIGH_ROW + 4, lanes] = value
    else:
        ref[16 * i + 14 : 16 * i + 16, lanes] = value[0:2]
        ref[16 * i : 16 * i + 2, lanes] = value[2:4]


def early_kernel(bands, c_ref, low_ref, high_ref, state, rows):
    low = low_ref[...].astype(f32)
    high = high_ref[...].astype(f32)
    for i in range(19):
        rows[16 * i + 10 : 16 * i + 14, :] = jnp.zeros((4, CELLS), f32)
        place_slab(rows, i, 0, c_ref[4 * i : 4 * i + 4, :], slice(None))
        place_slab(rows, i, -1, low[4 * i : 4 * i + 4], slice(None))
        place_slab(rows, i, 1, high[4 * i : 4 * i + 4], slice(None))
    for lo, hi, a, b in bands:
        lane = lax.broadcasted_iota(jnp.int32, (1, hi - lo), 1) + lo
        y, z = lane // PITCH - HALO, lane % PITCH - HALO
        inside = (y >= 0) & (y < BS) & (z >= 0) & (z < BS)
        source = jnp.where(inside, y * BS + z, -1)
        table = onehot(lax.broadcasted_iota(jnp.int32, (b - a, hi - lo), 0) + a == source)
        part = rows[:, a:b]
        coarse = part.astype(bf16)
        fine = (part - coarse.astype(f32)).astype(bf16)
        placed = jnp.dot(coarse, table, preferred_element_type=f32)
        state[:, lo:hi] = placed + jnp.dot(fine, table, preferred_element_type=f32)


def slots_kernel(slot_ref, geo_ref, hist_ref, table_ref, spec, notes, chosen):
    nt = (((1,), (1,)), ((), ()))
    spec[0:128, :] = lax.dot_general(table_ref[...], hist_ref[:, 0:256], nt, preferred_element_type=f32)
    spec[128:256, :] = lax.dot_general(table_ref[...], hist_ref[:, 256:512], nt, preferred_element_type=f32)
    newest = onehot(lax.broadcasted_iota(jnp.int32, (8, 256), 1) == SAMPLES - 1)
    notes[8:16, :] = lax.dot_general(newest, hist_ref[:, 0:256], nt, preferred_element_type=f32)
    cell, owner, count = slot_ref[0:1, :], slot_ref[1:2, :], slot_ref[2:3, :]
    step = lax.broadcasted_iota(jnp.int32, (64, 128), 0)
    which = onehot(step == owner // P_OWN)
    place = (step == owner % P_OWN).astype(f32)
    turned = (((0,), (0,)), ((), ()))
    picked = lax.dot_general(geo_ref[...], which, turned, preferred_element_type=f32)
    for c in range(6):
        notes[c : c + 1, :] = jnp.sum(picked[64 * c : 64 * c + 64] * place, axis=0, keepdims=True)
    notes[6:7, :] = count.astype(f32)
    notes[7:8, :] = (cell // CELLS).astype(f32)
    across = cell % CELLS
    spot = (across // BS + HALO) * PITCH + across % BS + HALO
    chosen[...] = onehot(lax.broadcasted_iota(jnp.int32, (LANES, 128), 0) == spot)


def flow_kernel(
    halo_bands, state_ref, own_ref, low_ref, high_ref, spec_ref, notes_ref, chosen_ref, late_ref,
    *rest,
):
    halo_refs = rest[: len(halo_bands)]
    out_ref, field_ref, packed, halo, here, there, seen = rest[len(halo_bands) :]
    lane4 = lax.broadcasted_iota(jnp.int32, (4, 128), 1)
    lane64 = lax.broadcasted_iota(jnp.int32, (64, 128), 1)
    for i in range(19):
        halo[16 * i + 10 : 16 * i + 14, :] = jnp.zeros((4, 640), f32)
    for slab, ref in ((0, own_ref), (-1, low_ref), (1, high_ref)):
        packed[...] = ref[...].astype(f32).reshape(512, 128)
        for face in range(4):
            inward, along, outward = classes(face)
            lanes = slice(face * 128, face * 128 + 128)

            def group(g):
                return packed[face * 64 + 4 * g : face * 64 + 4 * g + 4, :]

            for g, i in enumerate(inward + along):
                place_slab(halo, i, slab, group(g), lanes)
            for g, (a, b) in ((14, (0, 1)), (15, (2, 3))):
                place_slab(halo, outward[a], slab, group(g), lanes)
                place_slab(halo, outward[b], slab, pltpu.roll(group(g), 64, 1), lanes)
            last = jnp.where(lane4 < 32, pltpu.roll(group(5), 32, 1), pltpu.roll(group(6), 64, 1))
            place_slab(halo, outward[4], slab, last, lanes)
        corner = packed[256:320, :]
        for e in range(1, 4):
            corner = jnp.where((lane64 % 64) // 16 == e, packed[256 + 64 * e : 320 + 64 * e, :], corner)
        packed[256:320, :] = corner
        for i in range(19):
            rows = packed[256 + 4 * (i % 16) : 260 + 4 * (i % 16), :]
            rows = jnp.where((lane4 < 64) == (i < 16), rows, 0.0)
            place_slab(halo, i, slab, rows, slice(512, 640))
    for (lo, hi, a, b), halo_ref in zip(halo_bands, halo_refs):
        added = jnp.dot(halo[:, a:b].astype(bf16), halo_ref[...], preferred_element_type=f32)
        for i in range(19):
            here[i, :, lo:hi] = state_ref[16 * i : 16 * i + 16, lo:hi] + added[16 * i : 16 * i + 16] + WEIGHT[i]

    lane = lax.broadcasted_iota(jnp.int32, (1, LANES), 1)
    y, z = lane // PITCH - HALO, lane % PITCH - HALO
    inside = (y >= 0) & (y < BS) & (z >= 0) & (z < BS)
    for t in range(STEPS):
        depth_in = 16 if t < 2 else 8
        depth_out = 16 if t < 1 else 8
        for i, (cx, cy, cz) in enumerate(VEL):
            value = here[i, 0:depth_in, :]
            shift = (cy * PITCH + cz) % LANES
            if shift:
                value = pltpu.roll(value, shift, 1)
            if cx:
                value = pltpu.roll(value, cx % depth_in, 0)
            there[i, 0:depth_out, :] = value[0:depth_out]
        total = there[0, 0:8, :]
        for i in range(1, 19):
            total = total + there[i, 0:8, :]
        seen[8 * t : 8 * t + 8, :] = jnp.where(inside, total - 1.0, 0.0)
        if t < STEPS - 1:

            def one(c, _):
                at = pl.ds(pl.multiple_of(c * 128, 128), 128)
                for i, value in enumerate(collide([there[i, 0:depth_out, at] for i in range(19)])):
                    here[i, 0:depth_out, at] = value
                return 0

            lax.fori_loop(0, LANES // 128, one, 0)
    for i in range(19):
        field_ref[8 * i : 8 * i + 8, :] = jnp.where(inside, there[i, 0:8, :], 0.0)

    rest_of = seen[...]
    read = jnp.zeros((8 * STEPS, 128), f32)
    for _ in range(3):
        piece = rest_of.astype(bf16)
        read = read + jnp.dot(piece, chosen_ref[...], preferred_element_type=f32)
        rest_of = rest_of - piece.astype(f32)
    before = notes_ref[8:9, :]
    layer = notes_ref[7:8, :]
    press, rate = [], []
    for t in range(STEPS):
        value = jnp.zeros((1, 128), f32)
        for x in range(SLAB):
            row = 8 * t + OWN_ROW + x
            value = jnp.where(layer == x, read[row : row + 1], value)
        value = GAIN * value
        press.append(value.astype(bf16).astype(f32))
        rate.append((value - before).astype(bf16).astype(f32))
        before = value
    alive = lax.broadcasted_iota(jnp.int32, (1, 128), 1).astype(f32) < notes_ref[6:7, :]
    for g, late in ((0, press), (1, rate)):
        total = spec_ref[128 * g : 128 * g + 128, :]
        for t in range(STEPS):
            total = total + late_ref[:, t : t + 1] * late[t]
        out_ref[128 * g : 128 * g + 128, :] = jnp.where(alive, total, 0.0).astype(bf16)
    out_ref[256:272, :] = notes_ref[...].astype(bf16)


def field_kernel(bands, field_ref, *rest):
    own_refs, (out_ref,) = rest[: len(bands)], rest[len(bands) :]
    for (lo, hi, a, b), own_ref in zip(bands, own_refs):
        part = field_ref[:, a:b]
        coarse = part.astype(bf16)
        fine = (part - coarse.astype(f32)).astype(bf16)
        value = jnp.dot(coarse, own_ref[...], preferred_element_type=f32)
        value = value + jnp.dot(fine, own_ref[...], preferred_element_type=f32)
        for i in range(19):
            out_ref[0, i, :, lo:hi] = value[8 * i + OWN_ROW : 8 * i + OWN_ROW + 4]


def series(x, coefficients):
    value = coefficients[-1]
    for c in coefficients[-2::-1]:
        value = value * x + c
    return value


COSINE = [(-1.0) ** n / math.factorial(2 * n) for n in range(7)]
SINE = [(-1.0) ** n / math.factorial(2 * n + 1) for n in range(7)]
EARS = 32


def radiate_kernel(all_ref, listen_ref, out_ref, rows, spots, sums, goal):
    slot = lax.broadcasted_iota(jnp.int32, (128, 128), 0).astype(f32)
    base = jnp.zeros((1, 128), f32)
    for o in range(8):
        live = all_ref[o, 256:272, :].astype(f32)[6:7]
        goal[128 * o : 128 * o + 128, :] = jnp.where(slot < live, slot + base, -1.0)
        base = base + live
    used = jnp.max(base).astype(jnp.int32)
    everything = jnp.concatenate([all_ref[o] for o in range(8)], axis=1)
    for axis in range(3):
        spots[axis] = jnp.broadcast_to(listen_ref[axis : axis + 1, :], (128, 128)).T
    lane = lax.broadcasted_iota(jnp.int32, (1, 128), 1)

    lanes = lax.broadcasted_iota(jnp.int32, (EARS, 128), 1)

    def panels(p, first, final):
        here = onehot(goal[...] == (lane + 128 * p).astype(f32))
        rows[...] = jnp.dot(everything, here, preferred_element_type=f32)

        def listeners(m, _):
            ears = pl.ds(pl.multiple_of(m * EARS, EARS), EARS)
            distance_sq = jnp.zeros((EARS, 128), f32)
            facing = jnp.zeros((EARS, 128), f32)
            for axis in range(3):
                offset = spots[axis, ears, :] - rows[256 + axis : 257 + axis, :]
                distance_sq = distance_sq + offset * offset
                facing = facing + rows[259 + axis : 260 + axis, :] * offset
            distance = jnp.sqrt(distance_sq)
            far = facing / (4.0 * math.pi * SOUND * distance_sq)
            ratio = SOUND / distance
            angle = (2.0 * math.pi / SAMPLES) * (distance / SOUND)
            square = angle * angle
            cosine = series(square, COSINE)
            double = cosine + cosine
            c_before, s_before = far, jnp.zeros((EARS, 128), f32)
            c_now, s_now = far * cosine, far * (angle * series(square, SINE))
            result = jnp.zeros((EARS, 128), f32)
            for k in range(BINS):
                weight_real = rows[128 + k : 129 + k, :] + ratio * rows[k : k + 1, :]
                weight_imag = rows[192 + k : 193 + k, :] + ratio * rows[64 + k : 65 + k, :]
                real = weight_real * c_now + weight_imag * s_now
                imag = weight_imag * c_now - weight_real * s_now
                for n, value in ((k, real), (BINS + k, imag)):
                    at = slice(128 * n, 128 * n + 128)
                    if first:
                        sums[ears, at] = value
                    elif not final:
                        sums[ears, at] += value
                    else:
                        whole = jnp.sum(sums[ears, at] + value, axis=1, keepdims=True)
                        result = jnp.where(lanes == n, whole, result)
                if k < BINS - 1:
                    c_now, c_before = double * c_now - c_before, c_now
                    s_now, s_before = double * s_now - s_before, s_now
            if final:
                out_ref[ears, :] = result
            return 0

        lax.fori_loop(0, 128 // EARS, listeners, 0)
        return 0

    tiles = jnp.maximum((used + 127) // 128, 2)
    panels(0, True, False)
    lax.fori_loop(1, tiles - 1, lambda p, _: panels(p, False, False), 0)
    panels(tiles - 1, False, True)


def call(kernel, outs, operands, scratch=(), megabytes=32, flops=0):
    vmem = pl.BlockSpec(memory_space=pltpu.VMEM)
    return pl.pallas_call(
        kernel,
        out_shape=tuple(jax.ShapeDtypeStruct(s, d) for s, d in outs),
        in_specs=[vmem] * len(operands),
        out_specs=tuple(vmem for _ in outs),
        scratch_shapes=[pltpu.VMEM(s, f32) for s in scratch],
        compiler_params=pltpu.CompilerParams(vmem_limit_bytes=megabytes * 2**20),
        cost_estimate=pl.CostEstimate(flops=flops, bytes_accessed=2**20, transcendentals=0),
    )(*operands)


def body(
    populations,
    block_faces,
    block_edges,
    probe_cell,
    history,
    panel_count,
    panel_owner,
    panel_pos,
    panel_normal,
    observers,
):
    own = own_table()
    around = halo_table()
    bands = [(lo, hi, *band(own, lo, hi)) for lo, hi in tiles_of(LANES, 256)]
    halo_bands = [(lo, hi, *band(around, lo, hi)) for lo, hi in tiles_of(LANES, 256)]
    back = own.T
    back_bands = [(lo, hi, *band(back, lo, hi)) for lo, hi in tiles_of(CELLS, 256)]

    def cut(table, ranges):
        return [jnp.asarray(table[a:b, lo:hi].astype(jnp.bfloat16)) for lo, hi, a, b in ranges]

    table = transform_table()
    shifted = np.concatenate([np.zeros((STEPS, 128), table.dtype), table[: SAMPLES - STEPS]]).T
    late = np.zeros((128, 128), np.float32)
    late[:, :STEPS] = table[SAMPLES - STEPS :].astype(np.float32).T
    shapes = jnp.concatenate([panel_pos, panel_normal])
    links = jnp.concatenate([block_faces, block_edges])
    slot_facts = jnp.stack([probe_cell, panel_owner, jnp.broadcast_to(panel_count, probe_cell.shape)])
    collided, rounded, message = call(
        pack_kernel,
        [((80, CELLS), f32), ((80, CELLS), bf16), ((64, 16, 128), bf16)],
        [populations, shapes, links],
        scratch=[(80, 640), (320, 128), (64, 16, 128)],
    )
    ring = lax.axis_size("obs")
    up = [(i, (i + 1) % ring) for i in range(ring)]
    down = [(i, (i - 1) % ring) for i in range(ring)]

    def beside(value):
        return lax.ppermute(value, "obs", up), lax.ppermute(value, "obs", down)

    low, high = beside(rounded)
    spread = lax.all_to_all(message, "blk", 0, 0, tiled=True)
    sent, owners_geometry = call(
        forward_kernel,
        [((64, 8, 128), bf16), ((64, 384), bf16)],
        [spread],
        scratch=[(1024, 128), (512, 128)],
    )
    arrived = lax.all_to_all(sent, "blk", 0, 0, tiled=True)
    spec, notes, chosen = call(
        slots_kernel,
        [((256, 128), f32), ((16, 128), f32), ((LANES, 128), bf16)],
        [slot_facts, owners_geometry, history, jnp.asarray(shifted)],
        flops=10**8,
    )
    (state,) = call(
        functools.partial(early_kernel, bands),
        [((304, LANES), f32)],
        [collided, low, high],
        scratch=[(304, CELLS)],
        flops=10**8,
    )
    arrived, spec, notes, chosen = lax.optimization_barrier((arrived, spec, notes, chosen))
    arrived_low, arrived_high = beside(arrived)
    payload, field = call(
        functools.partial(flow_kernel, halo_bands),
        [((272, 128), bf16), ((152, LANES), f32)],
        [
            state, arrived, arrived_low, arrived_high, spec, notes, chosen, jnp.asarray(late),
            *cut(around, halo_bands),
        ],
        scratch=[(512, 128), (304, 640), (19, 16, LANES), (19, 16, LANES), (32, LANES)],
    )
    (populations_out,) = call(
        functools.partial(field_kernel, back_bands),
        [((1, 19, SLAB, CELLS), f32)],
        [field, *cut(back, back_bands)],
        flops=10**9,
    )
    gathered = lax.all_gather(payload, "obs", axis=0, tiled=False)
    (partial_value,) = call(
        radiate_kernel,
        [((128, 128), f32)],
        [gathered, observers],
        scratch=[(272, 128), (3, 128, 128), (128, 16384), (1024, 128)],
        megabytes=20,
    )
    pieces = lax.all_to_all(partial_value.reshape(64, 256), "blk", 0, 0, tiled=True)
    summed = jnp.sum(pieces, axis=0)
    return (populations_out, summed.reshape(1, 2, 2 * BINS))


def solution(mesh):
    placed = (
        P("blk", None, "obs", None),
        P("blk", None),
        P("blk", None),
        P(("blk", "obs")),
        P(("blk", "obs"), None),
        P(("blk", "obs")),
        P(("blk", "obs")),
        P(None, ("blk", "obs")),
        P(None, ("blk", "obs")),
        P(None, "obs"),
    )
    return jax.shard_map(
        body,
        mesh=mesh,
        in_specs=placed,
        out_specs=(P("blk", None, "obs", None), P("obs", "blk", None)),
        check_vma=False,
    )
```

```python
import functools
import math

import jax
import jax.numpy as jnp
import numpy as np
from jax import lax
from jax.experimental import pallas as pl
from jax.experimental.pallas import tpu as pltpu
from jax.sharding import PartitionSpec as P

BS = 32
STEPS = 4
SAMPLES = 256
BINS = 64
P_OWN = 64
SLAB = 4
CELLS = BS * BS
HALO = 4
PITCH = BS + 2 * HALO
LANES = 1664

VEL = [
    (0, 0, 0),
    (1, 0, 0),
    (-1, 0, 0),
    (0, 1, 0),
    (0, -1, 0),
    (0, 0, 1),
    (0, 0, -1),
    (1, 1, 0),
    (-1, -1, 0),
    (1, -1, 0),
    (-1, 1, 0),
    (1, 0, 1),
    (-1, 0, -1),
    (1, 0, -1),
    (-1, 0, 1),
    (0, 1, 1),
    (0, -1, -1),
    (0, 1, -1),
    (0, -1, 1),
]
WEIGHT = [1.0 / 3.0] + [1.0 / 18.0] * 6 + [1.0 / 36.0] * 12
PAIRS = [(1, 2), (3, 4), (5, 6), (7, 8), (9, 10), (11, 12), (13, 14), (15, 16), (17, 18)]
RELAX = 1.6
GAIN = 60.0
SOUND = 0.5
f32 = jnp.float32
bf16 = jnp.bfloat16

FACE_AXIS = [(1, -1), (1, 1), (2, -1), (2, 1)]


def classes(face):
    axis, sign = FACE_AXIS[face]
    inward = [i for i, v in enumerate(VEL) if v[axis] == sign]
    along = [i for i, v in enumerate(VEL) if v[axis] == 0]
    outward = [i for i, v in enumerate(VEL) if v[axis] == -sign]
    return inward, along, outward


def ext(y, z):
    return (y + HALO) * PITCH + z + HALO


def own_table():
    out = np.zeros((CELLS, LANES), np.float32)
    for y in range(BS):
        for z in range(BS):
            out[y * BS + z, ext(y, z)] = 1
    return out


def halo_table():
    out = np.zeros((640, LANES), np.float32)
    for d in range(HALO):
        for k in range(BS):
            out[d * BS + k, ext(BS + d, k)] = 1
            out[128 + d * BS + k, ext(-1 - d, k)] = 1
            out[256 + d * BS + k, ext(k, BS + d)] = 1
            out[384 + d * BS + k, ext(k, -1 - d)] = 1
    for e in range(4):
        for dy in range(HALO):
            for dz in range(HALO):
                y = BS + dy if e < 2 else -1 - dy
                z = BS + dz if e % 2 == 0 else -1 - dz
                lane = e * 16 + dy * HALO + dz
                out[512 + lane, ext(y, z)] = 1
                out[512 + 64 + lane, ext(y, z)] = 1
    return out


def tiles_of(total, step):
    return [(a, min(a + step, total)) for a in range(0, total, step)]


def band(table, lo, hi):
    rows = np.nonzero(table[:, lo:hi].any(axis=1))[0]
    if rows.size == 0:
        return 0, 128
    return int(rows[0]) // 128 * 128, -(-(int(rows[-1]) + 1) // 128) * 128


def transform_table():
    moments = np.arange(SAMPLES)[:, None]
    harmonics = np.arange(BINS)[None, :] + 1
    turns = moments * harmonics % SAMPLES
    phases = turns.astype(np.float32) * np.float32(2.0 * math.pi / SAMPLES)
    table = np.concatenate([np.cos(phases), -np.sin(phases)], axis=1).astype(np.float32)
    return table.astype(jnp.bfloat16)


def collide(fs):
    rho = fs[0]
    for f in fs[1:]:
        rho = rho + f
    speed = []
    for axis in range(3):
        up = [f for f, v in zip(fs, VEL) if v[axis] == 1]
        down = [f for f, v in zip(fs, VEL) if v[axis] == -1]
        speed.append(sum(up[1:], up[0]) - sum(down[1:], down[0]))
    inverse = 1.0 / rho
    speed = [s * inverse for s in speed]
    squared = speed[0] * speed[0] + speed[1] * speed[1] + speed[2] * speed[2]
    base = 1.0 - 1.5 * squared
    out = [None] * 19
    out[0] = (RELAX * WEIGHT[0]) * rho * base + (1.0 - RELAX) * fs[0]
    axis_scale = (RELAX / 18.0) * rho
    diagonal_scale = (RELAX / 36.0) * rho
    for a, b in PAIRS:
        along = None
        for axis in range(3):
            if VEL[a][axis] != 0:
                term = speed[axis]
                if along is None:
                    along = term if VEL[a][axis] == 1 else -term
                else:
                    along = along + term if VEL[a][axis] == 1 else along - term
        scale = axis_scale if a < 7 else diagonal_scale
        even = scale * (base + 4.5 * (along * along))
        odd = scale * (3.0 * along)
        out[a] = even + odd + (1.0 - RELAX) * fs[a]
        out[b] = even - odd + (1.0 - RELAX) * fs[b]
    return out


def strip_rows():
    lane = lax.broadcasted_iota(jnp.int32, (1, 128), 1)
    depth, along = lane // BS, lane % BS
    edge, dy, dz = lane // 16 % 4, lane // HALO % HALO, lane % HALO
    y = jnp.where(edge < 2, dy, BS - 1 - dy)
    z = jnp.where(edge % 2 == 0, dz, BS - 1 - dz)
    return jnp.concatenate([along * BS + depth, along * BS + BS - 1 - depth, y * BS + z], axis=1)


def onehot(condition):
    return condition.astype(f32).astype(bf16)


def face_groups(face):
    inward, along, outward = classes(face)
    upper = [(i, None) for i in inward] + [(outward[0], outward[1]), (outward[2], outward[3]), (along[8], None)]
    return upper, along[:8], outward[4]


def pack_kernel(*refs):
    given, made, refs = refs[:10], refs[10:15], refs[15:]
    here, ready, (strip, packed, came, gone) = refs[:10], refs[10:15], refs[15:]
    f_ref, faces, edges, count_ref, owner_ref, pos_ref, nor_ref, cell_ref, hist_ref, table_ref = here
    c_ref, cb_ref, msg_ref, spec, facts = ready
    arrivals = [pltpu.make_async_copy(a, b, came.at[n]) for n, (a, b) in enumerate(zip(given, here))]
    leaving = [pltpu.make_async_copy(a, b, gone.at[n]) for n, (a, b) in enumerate(zip(ready, made))]
    for copy in arrivals:
        copy.start()
    cell = lax.broadcasted_iota(jnp.int32, (CELLS, 384), 0)
    pick = onehot(cell == strip_rows())
    last = lax.broadcasted_iota(jnp.int32, (128, 128), 0)
    lane = lax.broadcasted_iota(jnp.int32, (128, 128), 1)
    turn = onehot(last == (HALO - 1 - lane // BS) * BS + lane % BS)
    for copy in arrivals:
        copy.wait()
    for lo, hi in tiles_of(CELLS, 256):
        fs = [f_ref[0, i, :, lo:hi] for i in range(19)]
        for i, c in enumerate(collide(fs)):
            c_ref[4 * i : 4 * i + 4, lo:hi] = c - WEIGHT[i]
    c_ref[76:80, :] = jnp.zeros((4, CELLS), f32)
    rounded = c_ref[...].astype(bf16)
    cb_ref[...] = rounded
    strip[:, 0:128] = rounded[:, 0:128].astype(f32)
    strip[:, 128:256] = jnp.dot(rounded[:, CELLS - 128 :], turn, preferred_element_type=f32)
    strip[:, 256:640] = jnp.dot(rounded, pick, preferred_element_type=f32)
    lane4 = lax.broadcasted_iota(jnp.int32, (4, 128), 1)
    row4 = lax.broadcasted_iota(jnp.int32, (4, 128), 0)
    for face in range(4):
        upper, lower, cut_up = face_groups(face)

        def rows(i):
            return strip[4 * i : 4 * i + 4, face * 128 : face * 128 + 128]

        near, next_to = pltpu.roll(rows(cut_up), 96, 1), pltpu.roll(rows(cut_up), 64, 1)
        for slot in range(8):
            at = face * 64 + 8 * slot
            a, b = upper[slot]
            value = rows(a)
            if b is not None:
                value = jnp.where(lane4 < 64, value, pltpu.roll(rows(b), 64, 1))
            packed[at : at + 4, :] = value
            piece = (near if slot < 4 else next_to)[slot % 4 : slot % 4 + 1]
            value = jnp.where((lane4 >= 96) & (row4 == 0), piece, rows(lower[slot]))
            packed[at + 4 : at + 8, :] = value
    packed[256:320, :] = strip[0:64, 512:640]
    for n in range(3):
        at = 256 + 8 * n
        packed[at : at + 4, :] = jnp.where(lane4 < 64, packed[at : at + 4, :], strip[64 + 4 * n : 68 + 4 * n, 512:640])
    for message in range(5, 8):
        packed[64 * message : 64 * message + 64, :] = packed[256:320, :]

    owner, count = owner_ref[...], count_ref[0]
    step = lax.broadcasted_iota(jnp.int32, (64, 128), 0)
    slot = lax.broadcasted_iota(jnp.int32, (1, 128), 1)
    asked = ((step == owner // P_OWN) & (slot < count)).astype(f32)
    turned = (((0,), (0,)), ((), ()))
    same = lax.dot_general(asked.astype(bf16), asked.astype(bf16), turned, preferred_element_type=f32)
    order = jnp.sum(jnp.where(last < lane, same, 0.0), axis=0, keepdims=True)
    place = (owner % P_OWN).astype(f32)
    kind = lax.broadcasted_iota(jnp.int32, (64, 1), 0) // 8
    source = jnp.zeros((64, 1), f32)
    for message in range(8):
        block = faces[0, (1, 0, 3, 2)[message]] if message < 4 else edges[0, 7 - message]
        source = jnp.where(kind == message, jnp.full((64, 1), block, jnp.int32).astype(f32), source)
    lane64 = lax.broadcasted_iota(jnp.int32, (64, 128), 1)
    extra = [source]
    for n in range(2):
        mine = jnp.where(order == n, asked, 0.0)
        facts[64 * n : 64 * n + 64, :] = mine
        extra.append(jnp.sum(mine * place, axis=1, keepdims=True))
    for n in range(3):
        at = pl.ds(5 + n, 64, stride=8)
        packed[at, :] = jnp.where(lane64 < 96, packed[at, :], extra[n])
    msg_ref[...] = packed[...].reshape(64, 8, 128).astype(bf16)
    for copy in leaving[:3]:
        copy.start()
    facts[136:160, :] = jnp.zeros((24, 128), f32)
    facts[144:147, 0:P_OWN] = pos_ref[...].astype(f32)
    facts[147:150, 0:P_OWN] = nor_ref[...].astype(f32)
    nt = (((1,), (1,)), ((), ()))
    spec[0:128, :] = lax.dot_general(table_ref[...], hist_ref[:, 0:256], nt, preferred_element_type=f32)
    spec[128:256, :] = lax.dot_general(table_ref[...], hist_ref[:, 256:512], nt, preferred_element_type=f32)
    newest = onehot(lax.broadcasted_iota(jnp.int32, (8, 256), 1) == SAMPLES - 1)
    facts[128:136, :] = lax.dot_general(newest, hist_ref[:, 0:256], nt, preferred_element_type=f32)
    spot = cell_ref[...]
    facts[136:137, :] = (spot // CELLS).astype(f32)
    facts[137:138, :] = jnp.full((1, 128), count, jnp.int32).astype(f32)
    across = spot % CELLS
    facts[138:139, :] = ((across // BS + HALO) * PITCH + across % BS + HALO).astype(f32)
    for copy in leaving[3:]:
        copy.start()
    for copy in leaving:
        copy.wait()


def forward_kernel(in_ref, facts_ref, out_ref, kept_ref, rows, moved, shape):
    rows[...] = in_ref[...].astype(f32).reshape(512, 128)

    def every(r):
        return rows[pl.ds(r, 64, stride=8), :]

    square = lax.broadcasted_iota(jnp.int32, (64, 64), 1).astype(f32)
    lane64 = lax.broadcasted_iota(jnp.int32, (64, 128), 1)
    mine = onehot(every(5)[:, 96:97] == square)
    sent = jnp.concatenate([every(r) for r in range(8)], axis=1).astype(bf16)
    picked = jnp.dot(mine, sent, preferred_element_type=f32)
    shape[...] = jnp.zeros((128, P_OWN), f32)
    shape[96:112, :] = facts_ref[144:160, 0:P_OWN]
    table = shape[...].astype(bf16)
    nt = (((1,), (1,)), ((), ()))
    for r in range(8):
        value = picked[:, 128 * r : 128 * r + 128]
        if r in (5, 6):
            question = onehot(every(r + 1)[:, 96:97] == square)
            answer = lax.dot_general(question, table, nt, preferred_element_type=f32)
            value = jnp.where(lane64 < 96, value, answer)
        moved[pl.ds(r, 64, stride=8), :] = value
    out_ref[...] = moved[...].reshape(64, 8, 128).astype(bf16)
    kept_ref[...] = facts_ref[...]


OWN_ROW, HIGH_ROW = 2, 6


def place_slab(ref, i, slab, value, lanes):
    if slab == 0:
        ref[16 * i + OWN_ROW : 16 * i + OWN_ROW + 4, lanes] = value
    elif slab == 1:
        ref[16 * i + HIGH_ROW : 16 * i + HIGH_ROW + 4, lanes] = value
    else:
        ref[16 * i + 14 : 16 * i + 16, lanes] = value[0:2]
        ref[16 * i : 16 * i + 2, lanes] = value[2:4]


def early_kernel(bands, c_ref, low_ref, high_ref, arrived_ref, facts_ref, state, notes, chosen, rows, answers):
    answers[...] = arrived_ref[...].astype(f32).reshape(512, 128)
    turned = (((0,), (0,)), ((), ()))
    found = jnp.zeros((128, 128), f32)
    for n in range(2):
        answer = answers[pl.ds(5 + n, 64, stride=8), :].astype(bf16)
        who = facts_ref[64 * n : 64 * n + 64, :].astype(bf16)
        found = found + lax.dot_general(answer, who, turned, preferred_element_type=f32)
    notes[0:8, :] = found[96:104]
    notes[8:24, :] = facts_ref[128:144, :]
    spot = facts_ref[138:139, :].astype(jnp.int32)
    chosen[...] = onehot(lax.broadcasted_iota(jnp.int32, (LANES, 128), 0) == spot)
    low = low_ref[...].astype(f32)
    high = high_ref[...].astype(f32)
    for i in range(19):
        rows[16 * i + 10 : 16 * i + 14, :] = jnp.zeros((4, CELLS), f32)
        place_slab(rows, i, 0, c_ref[4 * i : 4 * i + 4, :], slice(None))
        place_slab(rows, i, -1, low[4 * i : 4 * i + 4], slice(None))
        place_slab(rows, i, 1, high[4 * i : 4 * i + 4], slice(None))
    for lo, hi, a, b in bands:
        lane = lax.broadcasted_iota(jnp.int32, (1, hi - lo), 1) + lo
        y, z = lane // PITCH - HALO, lane % PITCH - HALO
        inside = (y >= 0) & (y < BS) & (z >= 0) & (z < BS)
        source = jnp.where(inside, y * BS + z, -1)
        table = onehot(lax.broadcasted_iota(jnp.int32, (b - a, hi - lo), 0) + a == source)
        part = rows[:, a:b]
        coarse = part.astype(bf16)
        fine = (part - coarse.astype(f32)).astype(bf16)
        placed = jnp.dot(coarse, table, preferred_element_type=f32)
        state[:, lo:hi] = placed + jnp.dot(fine, table, preferred_element_type=f32)


def halo_rows(lane):
    y, z = lane // PITCH - HALO, lane % PITCH - HALO
    dy = jnp.where(y < 0, -1 - y, y - BS)
    dz = jnp.where(z < 0, -1 - z, z - BS)
    middle_y, middle_z = (y >= 0) & (y < BS), (z >= 0) & (z < BS)
    edge = 2 * (y < 0).astype(jnp.int32) + (z < 0).astype(jnp.int32)
    row = 512 + edge * 16 + dy * HALO + dz
    row = jnp.where(middle_z, jnp.where(y < 0, 128, 0) + dy * BS + z, row)
    row = jnp.where(middle_y, jnp.where(z < 0, 384, 256) + dz * BS + y, row)
    return jnp.where((middle_y & middle_z) | (y >= BS + HALO), -1, row)


def flow_kernel(
    halo_bands, state_ref, own_ref, low_ref, high_ref, notes_ref, chosen_ref,
    out_ref, field_ref, packed, halo, here, there, seen, late,
):
    lane4 = lax.broadcasted_iota(jnp.int32, (4, 128), 1)
    lane64 = lax.broadcasted_iota(jnp.int32, (64, 128), 1)
    for i in range(19):
        halo[16 * i + 10 : 16 * i + 14, :] = jnp.zeros((4, 640), f32)
    for slab, ref in ((0, own_ref), (-1, low_ref), (1, high_ref)):
        packed[...] = ref[...].astype(f32).reshape(512, 128)
        for face in range(4):
            upper, lower, cut_up = face_groups(face)
            lanes = slice(face * 128, face * 128 + 128)
            for slot in range(8):
                at = face * 64 + 8 * slot
                a, b = upper[slot]
                place_slab(halo, a, slab, packed[at : at + 4, :], lanes)
                if b is not None:
                    place_slab(halo, b, slab, pltpu.roll(packed[at : at + 4, :], 64, 1), lanes)
                place_slab(halo, lower[slot], slab, packed[at + 4 : at + 8, :], lanes)
            near = packed[pl.ds(face * 64 + 4, 4, stride=8), :]
            next_to = packed[pl.ds(face * 64 + 36, 4, stride=8), :]
            value = jnp.where(lane4 < 32, pltpu.roll(near, 32, 1), pltpu.roll(next_to, 64, 1))
            place_slab(halo, cut_up, slab, value, lanes)
        corner = packed[256:320, :]
        for e in range(1, 4):
            corner = jnp.where((lane64 % 64) // 16 == e, packed[256 + 64 * e : 320 + 64 * e, :], corner)
        packed[256:320, :] = corner
        for i in range(19):
            at = 256 + (4 * i if i < 16 else 8 * (i - 16))
            rows = packed[at : at + 4, :]
            rows = jnp.where((lane4 < 64) == (i < 16), rows, 0.0)
            place_slab(halo, i, slab, rows, slice(512, 640))
    for lo, hi, a, b in halo_bands:
        source = halo_rows(lax.broadcasted_iota(jnp.int32, (1, hi - lo), 1) + lo)
        row = lax.broadcasted_iota(jnp.int32, (b - a, hi - lo), 0) + a
        match = row == source
        if b > 512:
            match = match | (row == jnp.where(source >= 512, source + 64, -1))
        added = jnp.dot(halo[:, a:b].astype(bf16), onehot(match), preferred_element_type=f32)
        for i in range(19):
            here[i, :, lo:hi] = state_ref[16 * i : 16 * i + 16, lo:hi] + added[16 * i : 16 * i + 16] + WEIGHT[i]

    lane = lax.broadcasted_iota(jnp.int32, (1, LANES), 1)
    y, z = lane // PITCH - HALO, lane % PITCH - HALO
    inside = (y >= 0) & (y < BS) & (z >= 0) & (z < BS)
    for t in range(STEPS):
        depth_in = 16 if t < 2 else 8
        depth_out = 16 if t < 1 else 8
        for i, (cx, cy, cz) in enumerate(VEL):
            value = here[i, 0:depth_in, :]
            shift = (cy * PITCH + cz) % LANES
            if shift:
                value = pltpu.roll(value, shift, 1)
            if cx:
                value = pltpu.roll(value, cx % depth_in, 0)
            there[i, 0:depth_out, :] = value[0:depth_out]
        total = there[0, 0:8, :]
        for i in range(1, 19):
            total = total + there[i, 0:8, :]
        seen[8 * t : 8 * t + 8, :] = jnp.where(inside, total - 1.0, 0.0)
        if t < STEPS - 1:

            def one(c, _):
                at = pl.ds(pl.multiple_of(c * 128, 128), 128)
                for i, value in enumerate(collide([there[i, 0:depth_out, at] for i in range(19)])):
                    here[i, 0:depth_out, at] = value
                return 0

            lax.fori_loop(0, LANES // 128, one, 0)
    for i in range(19):
        field_ref[8 * i : 8 * i + 8, :] = jnp.where(inside, there[i, 0:8, :], 0.0)

    rest_of = seen[...]
    read = jnp.zeros((8 * STEPS, 128), f32)
    for _ in range(3):
        piece = rest_of.astype(bf16)
        read = read + jnp.dot(piece, chosen_ref[...], preferred_element_type=f32)
        rest_of = rest_of - piece.astype(f32)
    before = notes_ref[8:9, :]
    layer = notes_ref[16:17, :]
    for t in range(STEPS):
        value = jnp.zeros((1, 128), f32)
        for x in range(SLAB):
            row = 8 * t + OWN_ROW + x
            value = jnp.where(layer == x, read[row : row + 1], value)
        value = GAIN * value
        late[t : t + 1, :] = value
        late[STEPS + t : STEPS + t + 1, :] = value - before
        before = value
    late[8:16, :] = notes_ref[0:8, :]
    late[14:15, :] = notes_ref[17:18, :]
    for o in range(8):
        out_ref[o] = late[...].astype(bf16)


def field_kernel(bands, field_ref, *rest):
    own_refs, (out_ref,) = rest[: len(bands)], rest[len(bands) :]
    for (lo, hi, a, b), own_ref in zip(bands, own_refs):
        part = field_ref[:, a:b]
        coarse = part.astype(bf16)
        fine = (part - coarse.astype(f32)).astype(bf16)
        value = jnp.dot(coarse, own_ref[...], preferred_element_type=f32)
        value = value + jnp.dot(fine, own_ref[...], preferred_element_type=f32)
        for i in range(19):
            out_ref[0, i, :, lo:hi] = value[8 * i + OWN_ROW : 8 * i + OWN_ROW + 4]


def series(x, coefficients):
    value = coefficients[-1]
    for c in coefficients[-2::-1]:
        value = value * x + c
    return value


COSINE = [(-1.0) ** n / math.factorial(2 * n) for n in range(7)]
SINE = [(-1.0) ** n / math.factorial(2 * n + 1) for n in range(7)]
EARS = 32


def radiate_kernel(
    spec_in, table_in, all_in, listen_in, out_ref,
    rows, spots, sums, goal, every, spec_ref, table_ref, all_ref, listen_ref, came,
):
    pairs = [(all_in, all_ref), (table_in, table_ref), (listen_in, listen_ref)]
    pairs += [(spec_in.at[o], spec_ref.at[o]) for o in range(8)]
    copies = [pltpu.make_async_copy(a, b, came.at[n]) for n, (a, b) in enumerate(pairs)]
    for copy in copies:
        copy.start()
    for copy in copies[:3]:
        copy.wait()
    slot = lax.broadcasted_iota(jnp.int32, (128, 128), 0).astype(f32)
    base = jnp.zeros((1, 128), f32)
    for o in range(8):
        at = slice(128 * o, 128 * o + 128)
        copies[3 + o].wait()
        late = all_ref[o].astype(f32)
        for g in range(2):
            total = spec_ref[o, 128 * g : 128 * g + 128, :]
            for t in range(STEPS):
                total = total + table_ref[:, t : t + 1] * late[STEPS * g + t : STEPS * g + t + 1]
            every[128 * g : 128 * g + 128, at] = total.astype(bf16)
        every[256:272, at] = all_ref[o]
        live = late[14:15]
        goal[at, :] = jnp.where(slot < live, slot + base, -1.0)
        base = base + live
    used = jnp.max(base).astype(jnp.int32)
    for axis in range(3):
        spots[axis] = jnp.broadcast_to(listen_ref[axis : axis + 1, :], (128, 128)).T
    lane = lax.broadcasted_iota(jnp.int32, (1, 128), 1)
    lanes = lax.broadcasted_iota(jnp.int32, (EARS, 128), 1)
    shape = (EARS // 8, 8, 128)

    def panels(p, first, final):
        here = onehot(goal[...] == (lane + 128 * p).astype(f32))
        flat = jnp.dot(every[...], here, preferred_element_type=f32)
        rows[...] = jnp.broadcast_to(flat[:, None, :], (272, 8, 128))

        def listeners(m, _):
            ears = pl.ds(pl.multiple_of(m * EARS, EARS), EARS)
            distance_sq = jnp.zeros(shape, f32)
            facing = jnp.zeros(shape, f32)
            for axis in range(3):
                offset = spots[axis, ears, :].reshape(shape) - rows[264 + axis]
                distance_sq = distance_sq + offset * offset
                facing = facing + rows[267 + axis] * offset
            distance = jnp.sqrt(distance_sq)
            far = facing / (4.0 * math.pi * SOUND * distance_sq)
            ratio = SOUND / distance
            angle = (2.0 * math.pi / SAMPLES) * (distance / SOUND)
            square = angle * angle
            cosine = series(square, COSINE)
            double = cosine + cosine
            c_before, s_before = far, jnp.zeros(shape, f32)
            c_now, s_now = far * cosine, far * (angle * series(square, SINE))
            result = jnp.zeros((EARS, 128), f32)
            for k in range(BINS):
                weight_real = rows[128 + k] + ratio * rows[k]
                weight_imag = rows[192 + k] + ratio * rows[64 + k]
                real = weight_real * c_now + weight_imag * s_now
                imag = weight_imag * c_now - weight_real * s_now
                for n, value in ((k, real), (BINS + k, imag)):
                    value = value.reshape(EARS, 128)
                    at = slice(128 * n, 128 * n + 128)
                    if first:
                        sums[ears, at] = value
                    elif not final:
                        sums[ears, at] += value
                    else:
                        whole = jnp.sum(sums[ears, at] + value, axis=1, keepdims=True)
                        result = jnp.where(lanes == n, whole, result)
                if k < BINS - 1:
                    c_now, c_before = double * c_now - c_before, c_now
                    s_now, s_before = double * s_now - s_before, s_now
            if final:
                out_ref[ears, :] = result
            return 0

        lax.fori_loop(0, 128 // EARS, listeners, 0)
        return 0

    tiles = jnp.maximum((used + 127) // 128, 2)
    panels(0, True, False)
    lax.fori_loop(1, tiles - 1, lambda p, _: panels(p, False, False), 0)
    panels(tiles - 1, False, True)


def call(kernel, outs, operands, scratch=(), megabytes=32, flops=0, fetch=False, store=False):
    vmem, anywhere = (pl.BlockSpec(memory_space=space) for space in (pltpu.VMEM, pl.ANY))
    block = anywhere if fetch else vmem
    return pl.pallas_call(
        kernel,
        out_shape=tuple(jax.ShapeDtypeStruct(s, d) for s, d in outs),
        in_specs=[block] * len(operands),
        out_specs=tuple(anywhere if store else vmem for _ in outs),
        scratch_shapes=[pltpu.VMEM(s, f32) if isinstance(s, tuple) else s for s in scratch],
        compiler_params=pltpu.CompilerParams(vmem_limit_bytes=megabytes * 2**20),
        cost_estimate=pl.CostEstimate(flops=flops, bytes_accessed=2**20, transcendentals=0),
    )(*operands)


def body(
    populations,
    block_faces,
    block_edges,
    probe_cell,
    history,
    panel_count,
    panel_owner,
    panel_pos,
    panel_normal,
    observers,
):
    own = own_table()
    around = halo_table()
    bands = [(lo, hi, *band(own, lo, hi)) for lo, hi in tiles_of(LANES, 256)]
    halo_bands = [(lo, hi, *band(around, lo, hi)) for lo, hi in tiles_of(LANES, 256)]
    back = own.T
    back_bands = [(lo, hi, *band(back, lo, hi)) for lo, hi in tiles_of(CELLS, 256)]

    def cut(table, ranges):
        return [jnp.asarray(table[a:b, lo:hi].astype(jnp.bfloat16)) for lo, hi, a, b in ranges]

    table = transform_table()
    shifted = np.concatenate([np.zeros((STEPS, 128), table.dtype), table[: SAMPLES - STEPS]]).T
    late = np.zeros((128, 128), np.float32)
    late[:, :STEPS] = table[SAMPLES - STEPS :].astype(np.float32).T
    operands = [
        populations,
        block_faces,
        block_edges,
        panel_count,
        panel_owner.reshape(1, 128),
        panel_pos,
        panel_normal,
        probe_cell.reshape(1, 128),
        history,
        jnp.asarray(shifted),
    ]
    results = [
        ((80, CELLS), f32),
        ((80, CELLS), bf16),
        ((64, 8, 128), bf16),
        ((256, 128), f32),
        ((160, 128), f32),
    ]
    collided, rounded, message, spec, facts = call(
        pack_kernel,
        results,
        operands,
        scratch=[
            (pltpu.SMEM if 0 < n < 4 else pltpu.VMEM)(a.shape, a.dtype) for n, a in enumerate(operands)
        ]
        + [pltpu.VMEM(s, d) for s, d in results]
        + [(80, 640), (512, 128), pltpu.SemaphoreType.DMA((10,)), pltpu.SemaphoreType.DMA((5,))],
        megabytes=60,
        fetch=True,
        store=True,
    )
    all_spec = lax.all_gather(spec, "obs", axis=0, tiled=False)
    ring = lax.axis_size("obs")
    up = [(i, (i + 1) % ring) for i in range(ring)]
    down = [(i, (i - 1) % ring) for i in range(ring)]

    def beside(value):
        return lax.ppermute(value, "obs", up), lax.ppermute(value, "obs", down)

    low, high = beside(rounded)
    spread = lax.all_to_all(message, "blk", 0, 0, tiled=True)
    sent, facts = call(
        forward_kernel,
        [((64, 8, 128), bf16), ((160, 128), f32)],
        [spread, facts],
        scratch=[(512, 128), (512, 128), (128, P_OWN)],
    )
    arrived = lax.all_to_all(sent, "blk", 0, 0, tiled=True)
    arrived_low, arrived_high = beside(arrived)
    state, notes, chosen = call(
        functools.partial(early_kernel, bands),
        [((304, LANES), f32), ((24, 128), f32), ((LANES, 128), bf16)],
        [collided, low, high, arrived, facts],
        scratch=[(304, CELLS), (512, 128)],
        flops=10**8,
    )
    payload, field = call(
        functools.partial(flow_kernel, halo_bands),
        [((8, 16, 128), bf16), ((152, LANES), f32)],
        [state, arrived, arrived_low, arrived_high, notes, chosen],
        scratch=[(512, 128), (304, 640), (19, 16, LANES), (19, 16, LANES), (32, LANES), (16, 128)],
    )
    (populations_out,) = call(
        functools.partial(field_kernel, back_bands),
        [((1, 19, SLAB, CELLS), f32)],
        [field, *cut(back, back_bands)],
        flops=10**9,
    )
    newest = lax.all_to_all(payload, "obs", 0, 0, tiled=True)
    (partial_value,) = call(
        radiate_kernel,
        [((128, 128), f32)],
        [all_spec, jnp.asarray(late), newest, observers],
        scratch=[
            (272, 8, 128),
            (3, 128, 128),
            (128, 16384),
            (1024, 128),
            pltpu.VMEM((272, 1024), bf16),
            (8, 256, 128),
            (128, 128),
            pltpu.VMEM((8, 16, 128), bf16),
            (3, 128),
            pltpu.SemaphoreType.DMA((11,)),
        ],
        megabytes=60,
        fetch=True,
    )
    pieces = lax.all_to_all(partial_value.reshape(64, 256), "blk", 0, 0, tiled=True)
    summed = jnp.sum(pieces, axis=0)
    return (populations_out, summed.reshape(1, 2, 2 * BINS))


def solution(mesh):
    placed = (
        P("blk", None, "obs", None),
        P("blk", None),
        P("blk", None),
        P(("blk", "obs")),
        P(("blk", "obs"), None),
        P(("blk", "obs")),
        P(("blk", "obs")),
        P(None, ("blk", "obs")),
        P(None, ("blk", "obs")),
        P(None, "obs"),
    )
    return jax.shard_map(
        body,
        mesh=mesh,
        in_specs=placed,
        out_specs=(P("blk", None, "obs", None), P("obs", "blk", None)),
        check_vma=False,
    )
```

```python
import functools
import math

import jax
import jax.numpy as jnp
import numpy as np
from jax import lax
from jax.experimental import pallas as pl
from jax.experimental.pallas import tpu as pltpu
from jax.sharding import PartitionSpec as P

BS = 32
STEPS = 4
SAMPLES = 256
BINS = 64
P_OWN = 64
SLAB = 4
CELLS = BS * BS
HALO = 4
PITCH = BS + 2 * HALO
LANES = 1664

VEL = [
    (0, 0, 0),
    (1, 0, 0),
    (-1, 0, 0),
    (0, 1, 0),
    (0, -1, 0),
    (0, 0, 1),
    (0, 0, -1),
    (1, 1, 0),
    (-1, -1, 0),
    (1, -1, 0),
    (-1, 1, 0),
    (1, 0, 1),
    (-1, 0, -1),
    (1, 0, -1),
    (-1, 0, 1),
    (0, 1, 1),
    (0, -1, -1),
    (0, 1, -1),
    (0, -1, 1),
]
WEIGHT = [1.0 / 3.0] + [1.0 / 18.0] * 6 + [1.0 / 36.0] * 12
PAIRS = [(1, 2), (3, 4), (5, 6), (7, 8), (9, 10), (11, 12), (13, 14), (15, 16), (17, 18)]
RELAX = 1.6
GAIN = 60.0
SOUND = 0.5
f32 = jnp.float32
bf16 = jnp.bfloat16

FACE_AXIS = [(1, -1), (1, 1), (2, -1), (2, 1)]


def classes(face):
    axis, sign = FACE_AXIS[face]
    inward = [i for i, v in enumerate(VEL) if v[axis] == sign]
    along = [i for i, v in enumerate(VEL) if v[axis] == 0]
    outward = [i for i, v in enumerate(VEL) if v[axis] == -sign]
    return inward, along, outward


def ext(y, z):
    return (y + HALO) * PITCH + z + HALO


def own_table():
    out = np.zeros((CELLS, LANES), np.float32)
    for y in range(BS):
        for z in range(BS):
            out[y * BS + z, ext(y, z)] = 1
    return out


def halo_table():
    out = np.zeros((640, LANES), np.float32)
    for d in range(HALO):
        for k in range(BS):
            out[d * BS + k, ext(BS + d, k)] = 1
            out[128 + d * BS + k, ext(-1 - d, k)] = 1
            out[256 + d * BS + k, ext(k, BS + d)] = 1
            out[384 + d * BS + k, ext(k, -1 - d)] = 1
    for e in range(4):
        for dy in range(HALO):
            for dz in range(HALO):
                y = BS + dy if e < 2 else -1 - dy
                z = BS + dz if e % 2 == 0 else -1 - dz
                lane = e * 16 + dy * HALO + dz
                out[512 + lane, ext(y, z)] = 1
                out[512 + 64 + lane, ext(y, z)] = 1
    return out


def tiles_of(total, step):
    return [(a, min(a + step, total)) for a in range(0, total, step)]


def band(table, lo, hi):
    rows = np.nonzero(table[:, lo:hi].any(axis=1))[0]
    if rows.size == 0:
        return 0, 128
    return int(rows[0]) // 128 * 128, -(-(int(rows[-1]) + 1) // 128) * 128


def transform_table():
    moments = np.arange(SAMPLES)[:, None]
    harmonics = np.arange(BINS)[None, :] + 1
    turns = moments * harmonics % SAMPLES
    phases = turns.astype(np.float32) * np.float32(2.0 * math.pi / SAMPLES)
    table = np.concatenate([np.cos(phases), -np.sin(phases)], axis=1).astype(np.float32)
    return table.astype(jnp.bfloat16)


def collide(fs):
    rho = fs[0]
    for f in fs[1:]:
        rho = rho + f
    speed = []
    for axis in range(3):
        up = [f for f, v in zip(fs, VEL) if v[axis] == 1]
        down = [f for f, v in zip(fs, VEL) if v[axis] == -1]
        speed.append(sum(up[1:], up[0]) - sum(down[1:], down[0]))
    inverse = 1.0 / rho
    speed = [s * inverse for s in speed]
    squared = speed[0] * speed[0] + speed[1] * speed[1] + speed[2] * speed[2]
    base = 1.0 - 1.5 * squared
    out = [None] * 19
    out[0] = (RELAX * WEIGHT[0]) * rho * base + (1.0 - RELAX) * fs[0]
    axis_scale = (RELAX / 18.0) * rho
    diagonal_scale = (RELAX / 36.0) * rho
    for a, b in PAIRS:
        along = None
        for axis in range(3):
            if VEL[a][axis] != 0:
                term = speed[axis]
                if along is None:
                    along = term if VEL[a][axis] == 1 else -term
                else:
                    along = along + term if VEL[a][axis] == 1 else along - term
        scale = axis_scale if a < 7 else diagonal_scale
        even = scale * (base + 4.5 * (along * along))
        odd = scale * (3.0 * along)
        out[a] = even + odd + (1.0 - RELAX) * fs[a]
        out[b] = even - odd + (1.0 - RELAX) * fs[b]
    return out


def strip_rows():
    lane = lax.broadcasted_iota(jnp.int32, (1, 128), 1)
    depth, along = lane // BS, lane % BS
    edge, dy, dz = lane // 16 % 4, lane // HALO % HALO, lane % HALO
    y = jnp.where(edge < 2, dy, BS - 1 - dy)
    z = jnp.where(edge % 2 == 0, dz, BS - 1 - dz)
    return jnp.concatenate([along * BS + depth, along * BS + BS - 1 - depth, y * BS + z], axis=1)


def onehot(condition):
    return condition.astype(f32).astype(bf16)


def face_groups(face):
    inward, along, outward = classes(face)
    upper = [(i, None) for i in inward] + [(outward[0], outward[1]), (outward[2], outward[3]), (along[8], None)]
    return upper, along[:8], outward[4]


def pack_kernel(*refs):
    given, made, refs = refs[:8], refs[8:12], refs[12:]
    here, ready, (strip, packed, came, gone) = refs[:8], refs[8:12], refs[12:]
    f_ref, faces, edges, count_ref, owner_ref, pos_ref, nor_ref, cell_ref = here
    c_ref, cb_ref, msg_ref, facts = ready
    arrivals = [pltpu.make_async_copy(a, b, came.at[n]) for n, (a, b) in enumerate(zip(given, here))]
    leaving = [pltpu.make_async_copy(a, b, gone.at[n]) for n, (a, b) in enumerate(zip(ready, made))]
    for copy in arrivals:
        copy.start()
    cell = lax.broadcasted_iota(jnp.int32, (CELLS, 384), 0)
    pick = onehot(cell == strip_rows())
    last = lax.broadcasted_iota(jnp.int32, (128, 128), 0)
    lane = lax.broadcasted_iota(jnp.int32, (128, 128), 1)
    turn = onehot(last == (HALO - 1 - lane // BS) * BS + lane % BS)
    for copy in arrivals:
        copy.wait()
    for lo, hi in tiles_of(CELLS, 256):
        fs = [f_ref[0, i, :, lo:hi] for i in range(19)]
        for i, c in enumerate(collide(fs)):
            c_ref[4 * i : 4 * i + 4, lo:hi] = c - WEIGHT[i]
    c_ref[76:80, :] = jnp.zeros((4, CELLS), f32)
    rounded = c_ref[...].astype(bf16)
    cb_ref[...] = rounded
    strip[:, 0:128] = rounded[:, 0:128].astype(f32)
    strip[:, 128:256] = jnp.dot(rounded[:, CELLS - 128 :], turn, preferred_element_type=f32)
    strip[:, 256:640] = jnp.dot(rounded, pick, preferred_element_type=f32)
    lane4 = lax.broadcasted_iota(jnp.int32, (4, 128), 1)
    row4 = lax.broadcasted_iota(jnp.int32, (4, 128), 0)
    for face in range(4):
        upper, lower, cut_up = face_groups(face)

        def rows(i):
            return strip[4 * i : 4 * i + 4, face * 128 : face * 128 + 128]

        near, next_to = pltpu.roll(rows(cut_up), 96, 1), pltpu.roll(rows(cut_up), 64, 1)
        for slot in range(8):
            at = face * 64 + 8 * slot
            a, b = upper[slot]
            value = rows(a)
            if b is not None:
                value = jnp.where(lane4 < 64, value, pltpu.roll(rows(b), 64, 1))
            packed[at : at + 4, :] = value
            piece = (near if slot < 4 else next_to)[slot % 4 : slot % 4 + 1]
            value = jnp.where((lane4 >= 96) & (row4 == 0), piece, rows(lower[slot]))
            packed[at + 4 : at + 8, :] = value
    packed[256:320, :] = strip[0:64, 512:640]
    for n in range(3):
        at = 256 + 8 * n
        packed[at : at + 4, :] = jnp.where(lane4 < 64, packed[at : at + 4, :], strip[64 + 4 * n : 68 + 4 * n, 512:640])
    for message in range(5, 8):
        packed[64 * message : 64 * message + 64, :] = packed[256:320, :]

    owner, count = owner_ref[...], count_ref[0]
    step = lax.broadcasted_iota(jnp.int32, (64, 128), 0)
    slot = lax.broadcasted_iota(jnp.int32, (1, 128), 1)
    asked = ((step == owner // P_OWN) & (slot < count)).astype(f32)
    turned = (((0,), (0,)), ((), ()))
    same = lax.dot_general(asked.astype(bf16), asked.astype(bf16), turned, preferred_element_type=f32)
    order = jnp.sum(jnp.where(last < lane, same, 0.0), axis=0, keepdims=True)
    place = (owner % P_OWN).astype(f32)
    kind = lax.broadcasted_iota(jnp.int32, (64, 1), 0) // 8
    source = jnp.zeros((64, 1), f32)
    for message in range(8):
        block = faces[0, (1, 0, 3, 2)[message]] if message < 4 else edges[0, 7 - message]
        source = jnp.where(kind == message, jnp.full((64, 1), block, jnp.int32).astype(f32), source)
    lane64 = lax.broadcasted_iota(jnp.int32, (64, 128), 1)
    extra = [source]
    for n in range(2):
        mine = jnp.where(order == n, asked, 0.0)
        facts[64 * n : 64 * n + 64, :] = mine
        extra.append(jnp.sum(mine * place, axis=1, keepdims=True))
    for n in range(3):
        at = pl.ds(5 + n, 64, stride=8)
        packed[at, :] = jnp.where(lane64 < 96, packed[at, :], extra[n])
    msg_ref[...] = packed[...].reshape(64, 8, 128).astype(bf16)
    for copy in leaving[:3]:
        copy.start()
    facts[128:160, :] = jnp.zeros((32, 128), f32)
    facts[144:147, 0:P_OWN] = pos_ref[...].astype(f32)
    facts[147:150, 0:P_OWN] = nor_ref[...].astype(f32)
    spot = cell_ref[...]
    facts[136:137, :] = (spot // CELLS).astype(f32)
    facts[137:138, :] = jnp.full((1, 128), count, jnp.int32).astype(f32)
    across = spot % CELLS
    facts[138:139, :] = ((across // BS + HALO) * PITCH + across % BS + HALO).astype(f32)
    for copy in leaving[3:]:
        copy.start()
    for copy in leaving:
        copy.wait()


def forward_kernel(in_ref, facts_ref, out_ref, kept_ref, rows, moved, shape):
    rows[...] = in_ref[...].astype(f32).reshape(512, 128)

    def every(r):
        return rows[pl.ds(r, 64, stride=8), :]

    square = lax.broadcasted_iota(jnp.int32, (64, 64), 1).astype(f32)
    lane64 = lax.broadcasted_iota(jnp.int32, (64, 128), 1)
    mine = onehot(every(5)[:, 96:97] == square)
    sent = jnp.concatenate([every(r) for r in range(8)], axis=1).astype(bf16)
    picked = jnp.dot(mine, sent, preferred_element_type=f32)
    shape[...] = jnp.zeros((128, P_OWN), f32)
    shape[96:112, :] = facts_ref[144:160, 0:P_OWN]
    table = shape[...].astype(bf16)
    nt = (((1,), (1,)), ((), ()))
    for r in range(8):
        value = picked[:, 128 * r : 128 * r + 128]
        if r in (5, 6):
            question = onehot(every(r + 1)[:, 96:97] == square)
            answer = lax.dot_general(question, table, nt, preferred_element_type=f32)
            value = jnp.where(lane64 < 96, value, answer)
        moved[pl.ds(r, 64, stride=8), :] = value
    out_ref[...] = moved[...].reshape(64, 8, 128).astype(bf16)
    kept_ref[...] = facts_ref[...]


OWN_ROW, HIGH_ROW = 2, 6


def place_slab(ref, i, slab, value, lanes):
    if slab == 0:
        ref[16 * i + OWN_ROW : 16 * i + OWN_ROW + 4, lanes] = value
    elif slab == 1:
        ref[16 * i + HIGH_ROW : 16 * i + HIGH_ROW + 4, lanes] = value
    else:
        ref[16 * i + 14 : 16 * i + 16, lanes] = value[0:2]
        ref[16 * i : 16 * i + 2, lanes] = value[2:4]


def slots_kernel(facts_ref, hist_ref, table_ref, late_ref, spec, late, chosen):
    nt = (((1,), (1,)), ((), ()))
    spec[0:128, :] = lax.dot_general(table_ref[...], hist_ref[:, 0:256], nt, preferred_element_type=f32)
    spec[128:256, :] = lax.dot_general(table_ref[...], hist_ref[:, 256:512], nt, preferred_element_type=f32)
    newest = onehot(lax.broadcasted_iota(jnp.int32, (8, 256), 1) == SAMPLES - 1)
    spec[256:264, :] = lax.dot_general(newest, hist_ref[:, 0:256], nt, preferred_element_type=f32)
    spec[264:272, :] = facts_ref[136:144, :]
    late[...] = late_ref[...]
    spot = facts_ref[138:139, :].astype(jnp.int32)
    chosen[...] = onehot(lax.broadcasted_iota(jnp.int32, (LANES, 128), 0) == spot)


def early_kernel(bands, c_ref, low_ref, high_ref, arrived_ref, facts_ref, state, geo, rows, answers):
    answers[...] = arrived_ref[...].astype(f32).reshape(512, 128)
    turned = (((0,), (0,)), ((), ()))
    found = jnp.zeros((128, 128), f32)
    for n in range(2):
        answer = answers[pl.ds(5 + n, 64, stride=8), :].astype(bf16)
        who = facts_ref[64 * n : 64 * n + 64, :].astype(bf16)
        found = found + lax.dot_general(answer, who, turned, preferred_element_type=f32)
    geo[...] = found[96:104]
    low = low_ref[...].astype(f32)
    high = high_ref[...].astype(f32)
    for i in range(19):
        rows[16 * i + 10 : 16 * i + 14, :] = jnp.zeros((4, CELLS), f32)
        place_slab(rows, i, 0, c_ref[4 * i : 4 * i + 4, :], slice(None))
        place_slab(rows, i, -1, low[4 * i : 4 * i + 4], slice(None))
        place_slab(rows, i, 1, high[4 * i : 4 * i + 4], slice(None))
    for lo, hi, a, b in bands:
        lane = lax.broadcasted_iota(jnp.int32, (1, hi - lo), 1) + lo
        y, z = lane // PITCH - HALO, lane % PITCH - HALO
        inside = (y >= 0) & (y < BS) & (z >= 0) & (z < BS)
        source = jnp.where(inside, y * BS + z, -1)
        table = onehot(lax.broadcasted_iota(jnp.int32, (b - a, hi - lo), 0) + a == source)
        part = rows[:, a:b]
        coarse = part.astype(bf16)
        fine = (part - coarse.astype(f32)).astype(bf16)
        placed = jnp.dot(coarse, table, preferred_element_type=f32)
        state[:, lo:hi] = placed + jnp.dot(fine, table, preferred_element_type=f32)


def halo_rows(lane):
    y, z = lane // PITCH - HALO, lane % PITCH - HALO
    dy = jnp.where(y < 0, -1 - y, y - BS)
    dz = jnp.where(z < 0, -1 - z, z - BS)
    middle_y, middle_z = (y >= 0) & (y < BS), (z >= 0) & (z < BS)
    edge = 2 * (y < 0).astype(jnp.int32) + (z < 0).astype(jnp.int32)
    row = 512 + edge * 16 + dy * HALO + dz
    row = jnp.where(middle_z, jnp.where(y < 0, 128, 0) + dy * BS + z, row)
    row = jnp.where(middle_y, jnp.where(z < 0, 384, 256) + dz * BS + y, row)
    return jnp.where((middle_y & middle_z) | (y >= BS + HALO), -1, row)


def flow_kernel(
    halo_bands, state_ref, own_ref, low_ref, high_ref, spec_ref, table_ref, chosen_ref, geo_ref,
    out_ref, field_ref, packed, halo, here, there, seen, late,
):
    lane4 = lax.broadcasted_iota(jnp.int32, (4, 128), 1)
    lane64 = lax.broadcasted_iota(jnp.int32, (64, 128), 1)
    for i in range(19):
        halo[16 * i + 10 : 16 * i + 14, :] = jnp.zeros((4, 640), f32)
    for slab, ref in ((0, own_ref), (-1, low_ref), (1, high_ref)):
        packed[...] = ref[...].astype(f32).reshape(512, 128)
        for face in range(4):
            upper, lower, cut_up = face_groups(face)
            lanes = slice(face * 128, face * 128 + 128)
            for slot in range(8):
                at = face * 64 + 8 * slot
                a, b = upper[slot]
                place_slab(halo, a, slab, packed[at : at + 4, :], lanes)
                if b is not None:
                    place_slab(halo, b, slab, pltpu.roll(packed[at : at + 4, :], 64, 1), lanes)
                place_slab(halo, lower[slot], slab, packed[at + 4 : at + 8, :], lanes)
            near = packed[pl.ds(face * 64 + 4, 4, stride=8), :]
            next_to = packed[pl.ds(face * 64 + 36, 4, stride=8), :]
            value = jnp.where(lane4 < 32, pltpu.roll(near, 32, 1), pltpu.roll(next_to, 64, 1))
            place_slab(halo, cut_up, slab, value, lanes)
        corner = packed[256:320, :]
        for e in range(1, 4):
            corner = jnp.where((lane64 % 64) // 16 == e, packed[256 + 64 * e : 320 + 64 * e, :], corner)
        packed[256:320, :] = corner
        for i in range(19):
            at = 256 + (4 * i if i < 16 else 8 * (i - 16))
            rows = packed[at : at + 4, :]
            rows = jnp.where((lane4 < 64) == (i < 16), rows, 0.0)
            place_slab(halo, i, slab, rows, slice(512, 640))
    for lo, hi, a, b in halo_bands:
        source = halo_rows(lax.broadcasted_iota(jnp.int32, (1, hi - lo), 1) + lo)
        row = lax.broadcasted_iota(jnp.int32, (b - a, hi - lo), 0) + a
        match = row == source
        if b > 512:
            match = match | (row == jnp.where(source >= 512, source + 64, -1))
        added = jnp.dot(halo[:, a:b].astype(bf16), onehot(match), preferred_element_type=f32)
        for i in range(19):
            here[i, :, lo:hi] = state_ref[16 * i : 16 * i + 16, lo:hi] + added[16 * i : 16 * i + 16] + WEIGHT[i]

    lane = lax.broadcasted_iota(jnp.int32, (1, LANES), 1)
    y, z = lane // PITCH - HALO, lane % PITCH - HALO
    inside = (y >= 0) & (y < BS) & (z >= 0) & (z < BS)
    for t in range(STEPS):
        depth_in = 16 if t < 2 else 8
        depth_out = 16 if t < 1 else 8
        for i, (cx, cy, cz) in enumerate(VEL):
            value = here[i, 0:depth_in, :]
            shift = (cy * PITCH + cz) % LANES
            if shift:
                value = pltpu.roll(value, shift, 1)
            if cx:
                value = pltpu.roll(value, cx % depth_in, 0)
            there[i, 0:depth_out, :] = value[0:depth_out]
        total = there[0, 0:8, :]
        for i in range(1, 19):
            total = total + there[i, 0:8, :]
        seen[8 * t : 8 * t + 8, :] = jnp.where(inside, total - 1.0, 0.0)
        if t < STEPS - 1:

            def one(c, _):
                at = pl.ds(pl.multiple_of(c * 128, 128), 128)
                for i, value in enumerate(collide([there[i, 0:depth_out, at] for i in range(19)])):
                    here[i, 0:depth_out, at] = value
                return 0

            lax.fori_loop(0, LANES // 128, one, 0)
    for i in range(19):
        field_ref[8 * i : 8 * i + 8, :] = jnp.where(inside, there[i, 0:8, :], 0.0)

    rest_of = seen[...]
    read = jnp.zeros((8 * STEPS, 128), f32)
    for _ in range(3):
        piece = rest_of.astype(bf16)
        read = read + jnp.dot(piece, chosen_ref[...], preferred_element_type=f32)
        rest_of = rest_of - piece.astype(f32)
    before = spec_ref[256:257, :]
    layer = spec_ref[264:265, :]
    news = [[], []]
    for t in range(STEPS):
        value = jnp.zeros((1, 128), f32)
        for x in range(SLAB):
            row = 8 * t + OWN_ROW + x
            value = jnp.where(layer == x, read[row : row + 1], value)
        value = GAIN * value
        news[0].append(value.astype(bf16).astype(f32))
        news[1].append((value - before).astype(bf16).astype(f32))
        before = value
    for g in range(2):
        total = spec_ref[128 * g : 128 * g + 128, :]
        for t in range(STEPS):
            total = total + table_ref[:, t : t + 1] * news[g][t]
        out_ref[128 * g : 128 * g + 128, :] = total.astype(bf16)
    late[0:8, :] = geo_ref[...]
    late[8:16, :] = spec_ref[264:272, :]
    out_ref[256:272, :] = late[...].astype(bf16)


def field_kernel(bands, field_ref, *rest):
    own_refs, (out_ref,) = rest[: len(bands)], rest[len(bands) :]
    for (lo, hi, a, b), own_ref in zip(bands, own_refs):
        part = field_ref[:, a:b]
        coarse = part.astype(bf16)
        fine = (part - coarse.astype(f32)).astype(bf16)
        value = jnp.dot(coarse, own_ref[...], preferred_element_type=f32)
        value = value + jnp.dot(fine, own_ref[...], preferred_element_type=f32)
        for i in range(19):
            out_ref[0, i, :, lo:hi] = value[8 * i + OWN_ROW : 8 * i + OWN_ROW + 4]


def series(x, coefficients):
    value = coefficients[-1]
    for c in coefficients[-2::-1]:
        value = value * x + c
    return value


COSINE = [(-1.0) ** n / math.factorial(2 * n) for n in range(7)]
SINE = [(-1.0) ** n / math.factorial(2 * n + 1) for n in range(7)]
EARS = 32


def radiate_kernel(all_ref, listen_ref, out_ref, rows, spots, sums, goal):
    slot = lax.broadcasted_iota(jnp.int32, (128, 128), 0).astype(f32)
    base = jnp.zeros((1, 128), f32)
    for o in range(8):
        live = all_ref[o, 256:272, :].astype(f32)[9:10]
        goal[128 * o : 128 * o + 128, :] = jnp.where(slot < live, slot + base, -1.0)
        base = base + live
    everything = jnp.concatenate([all_ref[o] for o in range(8)], axis=1)
    used = jnp.max(base).astype(jnp.int32)
    for axis in range(3):
        spots[axis] = jnp.broadcast_to(listen_ref[axis : axis + 1, :], (128, 128)).T
    lane = lax.broadcasted_iota(jnp.int32, (1, 128), 1)
    lanes = lax.broadcasted_iota(jnp.int32, (EARS, 128), 1)
    shape = (EARS // 8, 8, 128)

    def panels(p, first, final):
        here = onehot(goal[...] == (lane + 128 * p).astype(f32))
        flat = jnp.dot(everything, here, preferred_element_type=f32)
        rows[...] = jnp.broadcast_to(flat[:, None, :], (272, 8, 128))

        def listeners(m, _):
            ears = pl.ds(pl.multiple_of(m * EARS, EARS), EARS)
            distance_sq = jnp.zeros(shape, f32)
            facing = jnp.zeros(shape, f32)
            for axis in range(3):
                offset = spots[axis, ears, :].reshape(shape) - rows[256 + axis]
                distance_sq = distance_sq + offset * offset
                facing = facing + rows[259 + axis] * offset
            distance = jnp.sqrt(distance_sq)
            far = facing / (4.0 * math.pi * SOUND * distance_sq)
            ratio = SOUND / distance
            angle = (2.0 * math.pi / SAMPLES) * (distance / SOUND)
            square = angle * angle
            cosine = series(square, COSINE)
            double = cosine + cosine
            c_before, s_before = far, jnp.zeros(shape, f32)
            c_now, s_now = far * cosine, far * (angle * series(square, SINE))
            result = jnp.zeros((EARS, 128), f32)
            for k in range(BINS):
                weight_real = rows[128 + k] + ratio * rows[k]
                weight_imag = rows[192 + k] + ratio * rows[64 + k]
                real = weight_real * c_now + weight_imag * s_now
                imag = weight_imag * c_now - weight_real * s_now
                for n, value in ((k, real), (BINS + k, imag)):
                    value = value.reshape(EARS, 128)
                    at = slice(128 * n, 128 * n + 128)
                    if first:
                        sums[ears, at] = value
                    elif not final:
                        sums[ears, at] += value
                    else:
                        whole = jnp.sum(sums[ears, at] + value, axis=1, keepdims=True)
                        result = jnp.where(lanes == n, whole, result)
                if k < BINS - 1:
                    c_now, c_before = double * c_now - c_before, c_now
                    s_now, s_before = double * s_now - s_before, s_now
            if final:
                out_ref[ears, :] = result
            return 0

        lax.fori_loop(0, 128 // EARS, listeners, 0)
        return 0

    tiles = jnp.maximum((used + 127) // 128, 2)
    panels(0, True, False)
    lax.fori_loop(1, tiles - 1, lambda p, _: panels(p, False, False), 0)
    panels(tiles - 1, False, True)


def call(kernel, outs, operands, scratch=(), megabytes=32, flops=0, fetch=False, store=False):
    vmem, anywhere = (pl.BlockSpec(memory_space=space) for space in (pltpu.VMEM, pl.ANY))
    block = anywhere if fetch else vmem
    return pl.pallas_call(
        kernel,
        out_shape=tuple(jax.ShapeDtypeStruct(s, d) for s, d in outs),
        in_specs=[block] * len(operands),
        out_specs=tuple(anywhere if store else vmem for _ in outs),
        scratch_shapes=[pltpu.VMEM(s, f32) if isinstance(s, tuple) else s for s in scratch],
        compiler_params=pltpu.CompilerParams(vmem_limit_bytes=megabytes * 2**20),
        cost_estimate=pl.CostEstimate(flops=flops, bytes_accessed=2**20, transcendentals=0),
    )(*operands)


def body(
    populations,
    block_faces,
    block_edges,
    probe_cell,
    history,
    panel_count,
    panel_owner,
    panel_pos,
    panel_normal,
    observers,
):
    own = own_table()
    around = halo_table()
    bands = [(lo, hi, *band(own, lo, hi)) for lo, hi in tiles_of(LANES, 256)]
    halo_bands = [(lo, hi, *band(around, lo, hi)) for lo, hi in tiles_of(LANES, 256)]
    back = own.T
    back_bands = [(lo, hi, *band(back, lo, hi)) for lo, hi in tiles_of(CELLS, 256)]

    def cut(table, ranges):
        return [jnp.asarray(table[a:b, lo:hi].astype(jnp.bfloat16)) for lo, hi, a, b in ranges]

    table = transform_table()
    shifted = np.concatenate([np.zeros((STEPS, 128), table.dtype), table[: SAMPLES - STEPS]]).T
    late = np.zeros((128, 128), np.float32)
    late[:, :STEPS] = table[SAMPLES - STEPS :].astype(np.float32).T
    operands = [
        populations,
        block_faces,
        block_edges,
        panel_count,
        panel_owner.reshape(1, 128),
        panel_pos,
        panel_normal,
        probe_cell.reshape(1, 128),
    ]
    results = [
        ((80, CELLS), f32),
        ((80, CELLS), bf16),
        ((64, 8, 128), bf16),
        ((160, 128), f32),
    ]
    collided, rounded, message, facts = call(
        pack_kernel,
        results,
        operands,
        scratch=[
            (pltpu.SMEM if 0 < n < 4 else pltpu.VMEM)(a.shape, a.dtype) for n, a in enumerate(operands)
        ]
        + [pltpu.VMEM(s, d) for s, d in results]
        + [(80, 640), (512, 128), pltpu.SemaphoreType.DMA((8,)), pltpu.SemaphoreType.DMA((4,))],
        megabytes=60,
        fetch=True,
        store=True,
    )
    ring = lax.axis_size("obs")
    up = [(i, (i + 1) % ring) for i in range(ring)]
    down = [(i, (i - 1) % ring) for i in range(ring)]

    def beside(value):
        return lax.ppermute(value, "obs", up), lax.ppermute(value, "obs", down)

    low, high = beside(rounded)
    spread = lax.all_to_all(message, "blk", 0, 0, tiled=True)
    sent, facts = call(
        forward_kernel,
        [((64, 8, 128), bf16), ((160, 128), f32)],
        [spread, facts],
        scratch=[(512, 128), (512, 128), (128, P_OWN)],
    )
    arrived = lax.all_to_all(sent, "blk", 0, 0, tiled=True)
    spec, newest_table, chosen = call(
        slots_kernel,
        [((272, 128), f32), ((128, 128), f32), ((LANES, 128), bf16)],
        [facts, history, jnp.asarray(shifted), jnp.asarray(late)],
        flops=10**8,
    )
    arrived, spec, newest_table, chosen = lax.optimization_barrier((arrived, spec, newest_table, chosen))
    arrived_low, arrived_high = beside(arrived)
    state, geometry = call(
        functools.partial(early_kernel, bands),
        [((304, LANES), f32), ((8, 128), f32)],
        [collided, low, high, arrived, facts],
        scratch=[(304, CELLS), (512, 128)],
        flops=10**8,
    )
    payload, field = call(
        functools.partial(flow_kernel, halo_bands),
        [((272, 128), bf16), ((152, LANES), f32)],
        [state, arrived, arrived_low, arrived_high, spec, newest_table, chosen, geometry],
        scratch=[(512, 128), (304, 640), (19, 16, LANES), (19, 16, LANES), (32, LANES), (16, 128)],
    )
    (populations_out,) = call(
        functools.partial(field_kernel, back_bands),
        [((1, 19, SLAB, CELLS), f32)],
        [field, *cut(back, back_bands)],
        flops=10**9,
    )
    gathered = lax.all_gather(payload, "obs", axis=0, tiled=False)
    (partial_value,) = call(
        radiate_kernel,
        [((128, 128), f32)],
        [gathered, observers],
        scratch=[(272, 8, 128), (3, 128, 128), (128, 16384), (1024, 128)],
        megabytes=20,
    )
    pieces = lax.all_to_all(partial_value.reshape(64, 256), "blk", 0, 0, tiled=True)
    summed = jnp.sum(pieces, axis=0)
    return (populations_out, summed.reshape(1, 2, 2 * BINS))


def solution(mesh):
    placed = (
        P("blk", None, "obs", None),
        P("blk", None),
        P("blk", None),
        P(("blk", "obs")),
        P(("blk", "obs"), None),
        P(("blk", "obs")),
        P(("blk", "obs")),
        P(None, ("blk", "obs")),
        P(None, ("blk", "obs")),
        P(None, "obs"),
    )
    return jax.shard_map(
        body,
        mesh=mesh,
        in_specs=placed,
        out_specs=(P("blk", None, "obs", None), P("obs", "blk", None)),
        check_vma=False,
    )
```

```python
import functools
import math

import jax
import jax.numpy as jnp
import numpy as np
from jax import lax
from jax.experimental import pallas as pl
from jax.experimental.pallas import tpu as pltpu
from jax.sharding import PartitionSpec as P

BS = 32
STEPS = 4
SAMPLES = 256
BINS = 64
P_OWN = 64
SLAB = 4
CELLS = BS * BS
HALO = 4
PITCH = BS + 2 * HALO
LANES = 1664

VEL = [
    (0, 0, 0),
    (1, 0, 0),
    (-1, 0, 0),
    (0, 1, 0),
    (0, -1, 0),
    (0, 0, 1),
    (0, 0, -1),
    (1, 1, 0),
    (-1, -1, 0),
    (1, -1, 0),
    (-1, 1, 0),
    (1, 0, 1),
    (-1, 0, -1),
    (1, 0, -1),
    (-1, 0, 1),
    (0, 1, 1),
    (0, -1, -1),
    (0, 1, -1),
    (0, -1, 1),
]
WEIGHT = [1.0 / 3.0] + [1.0 / 18.0] * 6 + [1.0 / 36.0] * 12
PAIRS = [(1, 2), (3, 4), (5, 6), (7, 8), (9, 10), (11, 12), (13, 14), (15, 16), (17, 18)]
RELAX = 1.6
GAIN = 60.0
SOUND = 0.5
f32 = jnp.float32
bf16 = jnp.bfloat16

FACE_AXIS = [(1, -1), (1, 1), (2, -1), (2, 1)]


def classes(face):
    axis, sign = FACE_AXIS[face]
    inward = [i for i, v in enumerate(VEL) if v[axis] == sign]
    along = [i for i, v in enumerate(VEL) if v[axis] == 0]
    outward = [i for i, v in enumerate(VEL) if v[axis] == -sign]
    return inward, along, outward


def ext(y, z):
    return (y + HALO) * PITCH + z + HALO


def own_table():
    out = np.zeros((CELLS, LANES), np.float32)
    for y in range(BS):
        for z in range(BS):
            out[y * BS + z, ext(y, z)] = 1
    return out


def halo_table():
    out = np.zeros((640, LANES), np.float32)
    for d in range(HALO):
        for k in range(BS):
            out[d * BS + k, ext(BS + d, k)] = 1
            out[128 + d * BS + k, ext(-1 - d, k)] = 1
            out[256 + d * BS + k, ext(k, BS + d)] = 1
            out[384 + d * BS + k, ext(k, -1 - d)] = 1
    for e in range(4):
        for dy in range(HALO):
            for dz in range(HALO):
                y = BS + dy if e < 2 else -1 - dy
                z = BS + dz if e % 2 == 0 else -1 - dz
                lane = e * 16 + dy * HALO + dz
                out[512 + lane, ext(y, z)] = 1
                out[512 + 64 + lane, ext(y, z)] = 1
    return out


def tiles_of(total, step):
    return [(a, min(a + step, total)) for a in range(0, total, step)]


def band(table, lo, hi):
    rows = np.nonzero(table[:, lo:hi].any(axis=1))[0]
    if rows.size == 0:
        return 0, 128
    return int(rows[0]) // 128 * 128, -(-(int(rows[-1]) + 1) // 128) * 128


def transform_table():
    moments = np.arange(SAMPLES)[:, None]
    harmonics = np.arange(BINS)[None, :] + 1
    turns = moments * harmonics % SAMPLES
    phases = turns.astype(np.float32) * np.float32(2.0 * math.pi / SAMPLES)
    table = np.concatenate([np.cos(phases), -np.sin(phases)], axis=1).astype(np.float32)
    return table.astype(jnp.bfloat16)


def collide(fs):
    rho = fs[0]
    for f in fs[1:]:
        rho = rho + f
    between = [fs[a] - fs[b] for a, b in PAIRS]
    triple = 3.0 / rho
    fast = []
    for axis in range(3):
        momentum = None
        for (a, _), value in zip(PAIRS, between):
            if VEL[a][axis] == 1:
                momentum = value if momentum is None else momentum + value
            elif VEL[a][axis] == -1:
                momentum = momentum - value
        fast.append(momentum * triple)
    squared = fast[0] * fast[0] + fast[1] * fast[1] + fast[2] * fast[2]
    base = 2.0 - (1.0 / 3.0) * squared
    scales = [(RELAX / 18.0) * rho, (RELAX / 36.0) * rho, (RELAX / 72.0) * rho]
    out = [None] * 19
    out[0] = (0.5 * RELAX * WEIGHT[0]) * rho * base + (1.0 - RELAX) * fs[0]
    for a, b in PAIRS:
        along = None
        for axis in range(3):
            if VEL[a][axis] == 1:
                along = fast[axis] if along is None else along + fast[axis]
            elif VEL[a][axis] == -1:
                along = along - fast[axis]
        full, half = scales[:2] if a < 7 else scales[1:]
        even = half * (base + along * along)
        odd = full * along
        out[a] = (even + odd) + (1.0 - RELAX) * fs[a]
        out[b] = (even - odd) + (1.0 - RELAX) * fs[b]
    return out


def strip_rows():
    lane = lax.broadcasted_iota(jnp.int32, (1, 128), 1)
    depth, along = lane // BS, lane % BS
    edge, dy, dz = lane // 16 % 4, lane // HALO % HALO, lane % HALO
    y = jnp.where(edge < 2, dy, BS - 1 - dy)
    z = jnp.where(edge % 2 == 0, dz, BS - 1 - dz)
    return jnp.concatenate([along * BS + depth, along * BS + BS - 1 - depth, y * BS + z], axis=1)


def onehot(condition):
    return condition.astype(f32).astype(bf16)


def face_groups(face):
    inward, along, outward = classes(face)
    upper = [(i, None) for i in inward] + [(outward[0], outward[1]), (outward[2], outward[3]), (along[8], None)]
    return upper, along[:8], outward[4]


def pack_kernel(*refs):
    given, made, refs = refs[:8], refs[8:12], refs[12:]
    here, ready, (strip, packed, came, gone) = refs[:8], refs[8:12], refs[12:]
    f_ref, faces, edges, count_ref, owner_ref, pos_ref, nor_ref, cell_ref = here
    c_ref, cb_ref, msg_ref, facts = ready
    arrivals = [pltpu.make_async_copy(a, b, came.at[n]) for n, (a, b) in enumerate(zip(given, here))]
    leaving = [pltpu.make_async_copy(a, b, gone.at[n]) for n, (a, b) in enumerate(zip(ready, made))]
    for copy in arrivals:
        copy.start()
    cell = lax.broadcasted_iota(jnp.int32, (CELLS, 384), 0)
    pick = onehot(cell == strip_rows())
    last = lax.broadcasted_iota(jnp.int32, (128, 128), 0)
    lane = lax.broadcasted_iota(jnp.int32, (128, 128), 1)
    turn = onehot(last == (HALO - 1 - lane // BS) * BS + lane % BS)
    for copy in arrivals:
        copy.wait()
    for lo, hi in tiles_of(CELLS, 256):
        fs = [f_ref[0, i, :, lo:hi] for i in range(19)]
        for i, c in enumerate(collide(fs)):
            c_ref[4 * i : 4 * i + 4, lo:hi] = c - WEIGHT[i]
    c_ref[76:80, :] = jnp.zeros((4, CELLS), f32)
    rounded = c_ref[...].astype(bf16)
    cb_ref[...] = rounded
    strip[:, 0:128] = rounded[:, 0:128].astype(f32)
    strip[:, 128:256] = jnp.dot(rounded[:, CELLS - 128 :], turn, preferred_element_type=f32)
    strip[:, 256:640] = jnp.dot(rounded, pick, preferred_element_type=f32)
    lane4 = lax.broadcasted_iota(jnp.int32, (4, 128), 1)
    row4 = lax.broadcasted_iota(jnp.int32, (4, 128), 0)
    for face in range(4):
        upper, lower, cut_up = face_groups(face)

        def rows(i):
            return strip[4 * i : 4 * i + 4, face * 128 : face * 128 + 128]

        near, next_to = pltpu.roll(rows(cut_up), 96, 1), pltpu.roll(rows(cut_up), 64, 1)
        for slot in range(8):
            at = face * 64 + 8 * slot
            a, b = upper[slot]
            value = rows(a)
            if b is not None:
                value = jnp.where(lane4 < 64, value, pltpu.roll(rows(b), 64, 1))
            packed[at : at + 4, :] = value
            piece = (near if slot < 4 else next_to)[slot % 4 : slot % 4 + 1]
            value = jnp.where((lane4 >= 96) & (row4 == 0), piece, rows(lower[slot]))
            packed[at + 4 : at + 8, :] = value
    packed[256:320, :] = strip[0:64, 512:640]
    for n in range(3):
        at = 256 + 8 * n
        packed[at : at + 4, :] = jnp.where(lane4 < 64, packed[at : at + 4, :], strip[64 + 4 * n : 68 + 4 * n, 512:640])
    for message in range(5, 8):
        packed[64 * message : 64 * message + 64, :] = packed[256:320, :]

    owner, count = owner_ref[...], count_ref[0]
    step = lax.broadcasted_iota(jnp.int32, (64, 128), 0)
    slot = lax.broadcasted_iota(jnp.int32, (1, 128), 1)
    asked = ((step == owner // P_OWN) & (slot < count)).astype(f32)
    turned = (((0,), (0,)), ((), ()))
    same = lax.dot_general(asked.astype(bf16), asked.astype(bf16), turned, preferred_element_type=f32)
    order = jnp.sum(jnp.where(last < lane, same, 0.0), axis=0, keepdims=True)
    place = (owner % P_OWN).astype(f32)
    kind = lax.broadcasted_iota(jnp.int32, (64, 1), 0) // 8
    source = jnp.zeros((64, 1), f32)
    for message in range(8):
        block = faces[0, (1, 0, 3, 2)[message]] if message < 4 else edges[0, 7 - message]
        source = jnp.where(kind == message, jnp.full((64, 1), block, jnp.int32).astype(f32), source)
    lane64 = lax.broadcasted_iota(jnp.int32, (64, 128), 1)
    extra = [source]
    for n in range(2):
        mine = jnp.where(order == n, asked, 0.0)
        facts[64 * n : 64 * n + 64, :] = mine
        extra.append(jnp.sum(mine * place, axis=1, keepdims=True))
    for n in range(3):
        at = pl.ds(5 + n, 64, stride=8)
        packed[at, :] = jnp.where(lane64 < 96, packed[at, :], extra[n])
    msg_ref[...] = packed[...].reshape(64, 8, 128).astype(bf16)
    for copy in leaving[:3]:
        copy.start()
    facts[128:160, :] = jnp.zeros((32, 128), f32)
    facts[144:147, 0:P_OWN] = pos_ref[...].astype(f32)
    facts[147:150, 0:P_OWN] = nor_ref[...].astype(f32)
    spot = cell_ref[...]
    facts[136:137, :] = (spot // CELLS).astype(f32)
    facts[137:138, :] = jnp.full((1, 128), count, jnp.int32).astype(f32)
    across = spot % CELLS
    facts[138:139, :] = ((across // BS + HALO) * PITCH + across % BS + HALO).astype(f32)
    for copy in leaving[3:]:
        copy.start()
    for copy in leaving:
        copy.wait()


def forward_kernel(in_ref, facts_ref, out_ref, kept_ref, rows, moved, shape):
    rows[...] = in_ref[...].astype(f32).reshape(512, 128)

    def every(r):
        return rows[pl.ds(r, 64, stride=8), :]

    square = lax.broadcasted_iota(jnp.int32, (64, 64), 1).astype(f32)
    lane64 = lax.broadcasted_iota(jnp.int32, (64, 128), 1)
    mine = onehot(every(5)[:, 96:97] == square)
    sent = jnp.concatenate([every(r) for r in range(8)], axis=1).astype(bf16)
    picked = jnp.dot(mine, sent, preferred_element_type=f32)
    shape[...] = jnp.zeros((128, P_OWN), f32)
    shape[96:112, :] = facts_ref[144:160, 0:P_OWN]
    table = shape[...].astype(bf16)
    nt = (((1,), (1,)), ((), ()))
    for r in range(8):
        value = picked[:, 128 * r : 128 * r + 128]
        if r in (5, 6):
            question = onehot(every(r + 1)[:, 96:97] == square)
            answer = lax.dot_general(question, table, nt, preferred_element_type=f32)
            value = jnp.where(lane64 < 96, value, answer)
        moved[pl.ds(r, 64, stride=8), :] = value
    out_ref[...] = moved[...].reshape(64, 8, 128).astype(bf16)
    kept_ref[...] = facts_ref[...]


OWN_ROW, HIGH_ROW = 2, 6


def place_slab(ref, i, slab, value, lanes):
    if slab == 0:
        ref[16 * i + OWN_ROW : 16 * i + OWN_ROW + 4, lanes] = value
    elif slab == 1:
        ref[16 * i + HIGH_ROW : 16 * i + HIGH_ROW + 4, lanes] = value
    else:
        ref[16 * i + 14 : 16 * i + 16, lanes] = value[0:2]
        ref[16 * i : 16 * i + 2, lanes] = value[2:4]


def halo_rows(lane):
    y, z = lane // PITCH - HALO, lane % PITCH - HALO
    dy = jnp.where(y < 0, -1 - y, y - BS)
    dz = jnp.where(z < 0, -1 - z, z - BS)
    middle_y, middle_z = (y >= 0) & (y < BS), (z >= 0) & (z < BS)
    edge = 2 * (y < 0).astype(jnp.int32) + (z < 0).astype(jnp.int32)
    row = 512 + edge * 16 + dy * HALO + dz
    row = jnp.where(middle_z, jnp.where(y < 0, 128, 0) + dy * BS + z, row)
    row = jnp.where(middle_y, jnp.where(z < 0, 384, 256) + dz * BS + y, row)
    return jnp.where((middle_y & middle_z) | (y >= BS + HALO), -1, row)


def slots_kernel(halo_bands, facts_ref, hist_ref, table_ref, late_ref, spec, late, chosen, *tables):
    nt = (((1,), (1,)), ((), ()))
    spec[0:128, :] = lax.dot_general(table_ref[...], hist_ref[:, 0:256], nt, preferred_element_type=f32)
    spec[128:256, :] = lax.dot_general(table_ref[...], hist_ref[:, 256:512], nt, preferred_element_type=f32)
    newest = onehot(lax.broadcasted_iota(jnp.int32, (8, 256), 1) == SAMPLES - 1)
    spec[256:264, :] = lax.dot_general(newest, hist_ref[:, 0:256], nt, preferred_element_type=f32)
    spec[264:272, :] = facts_ref[136:144, :]
    late[...] = late_ref[...]
    spot = facts_ref[138:139, :].astype(jnp.int32)
    chosen[...] = onehot(lax.broadcasted_iota(jnp.int32, (LANES, 128), 0) == spot)
    for (lo, hi, a, b), table in zip(halo_bands, tables):
        source = halo_rows(lax.broadcasted_iota(jnp.int32, (1, hi - lo), 1) + lo)
        row = lax.broadcasted_iota(jnp.int32, (b - a, hi - lo), 0) + a
        match = row == source
        if b > 512:
            match = match | (row == jnp.where(source >= 512, source + 64, -1))
        table[...] = onehot(match)


def early_kernel(bands, c_ref, low_ref, high_ref, arrived_ref, facts_ref, state, geo, rows, answers):
    answers[...] = arrived_ref[...].astype(f32).reshape(512, 128)
    turned = (((0,), (0,)), ((), ()))
    found = jnp.zeros((128, 128), f32)
    for n in range(2):
        answer = answers[pl.ds(5 + n, 64, stride=8), :].astype(bf16)
        who = facts_ref[64 * n : 64 * n + 64, :].astype(bf16)
        found = found + lax.dot_general(answer, who, turned, preferred_element_type=f32)
    geo[...] = found[96:104]
    low = low_ref[...].astype(f32)
    high = high_ref[...].astype(f32)
    for i in range(19):
        rows[16 * i + 10 : 16 * i + 14, :] = jnp.zeros((4, CELLS), f32)
        place_slab(rows, i, 0, c_ref[4 * i : 4 * i + 4, :], slice(None))
        place_slab(rows, i, -1, low[4 * i : 4 * i + 4], slice(None))
        place_slab(rows, i, 1, high[4 * i : 4 * i + 4], slice(None))
    for lo, hi, a, b in bands:
        lane = lax.broadcasted_iota(jnp.int32, (1, hi - lo), 1) + lo
        y, z = lane // PITCH - HALO, lane % PITCH - HALO
        inside = (y >= 0) & (y < BS) & (z >= 0) & (z < BS)
        source = jnp.where(inside, y * BS + z, -1)
        table = onehot(lax.broadcasted_iota(jnp.int32, (b - a, hi - lo), 0) + a == source)
        part = rows[:, a:b]
        coarse = part.astype(bf16)
        fine = (part - coarse.astype(f32)).astype(bf16)
        placed = jnp.dot(coarse, table, preferred_element_type=f32)
        state[:, lo:hi] = placed + jnp.dot(fine, table, preferred_element_type=f32)


def flow_kernel(
    halo_bands, state_ref, own_ref, low_ref, high_ref, spec_ref, table_ref, chosen_ref, geo_ref, *rest,
):
    tables, rest = rest[: len(halo_bands)], rest[len(halo_bands) :]
    out_ref, field_ref, packed, halo, here, there, seen, late = rest
    lane4 = lax.broadcasted_iota(jnp.int32, (4, 128), 1)
    lane64 = lax.broadcasted_iota(jnp.int32, (64, 128), 1)
    for i in range(19):
        halo[16 * i + 10 : 16 * i + 14, :] = jnp.zeros((4, 640), f32)
    for slab, ref in ((0, own_ref), (-1, low_ref), (1, high_ref)):
        packed[...] = ref[...].astype(f32).reshape(512, 128)
        for face in range(4):
            upper, lower, cut_up = face_groups(face)
            lanes = slice(face * 128, face * 128 + 128)
            for slot in range(8):
                at = face * 64 + 8 * slot
                a, b = upper[slot]
                place_slab(halo, a, slab, packed[at : at + 4, :], lanes)
                if b is not None:
                    place_slab(halo, b, slab, pltpu.roll(packed[at : at + 4, :], 64, 1), lanes)
                place_slab(halo, lower[slot], slab, packed[at + 4 : at + 8, :], lanes)
            near = packed[pl.ds(face * 64 + 4, 4, stride=8), :]
            next_to = packed[pl.ds(face * 64 + 36, 4, stride=8), :]
            value = jnp.where(lane4 < 32, pltpu.roll(near, 32, 1), pltpu.roll(next_to, 64, 1))
            place_slab(halo, cut_up, slab, value, lanes)
        corner = packed[256:320, :]
        for e in range(1, 4):
            corner = jnp.where((lane64 % 64) // 16 == e, packed[256 + 64 * e : 320 + 64 * e, :], corner)
        packed[256:320, :] = corner
        for i in range(19):
            at = 256 + (4 * i if i < 16 else 8 * (i - 16))
            rows = packed[at : at + 4, :]
            rows = jnp.where((lane4 < 64) == (i < 16), rows, 0.0)
            place_slab(halo, i, slab, rows, slice(512, 640))
    for (lo, hi, a, b), table in zip(halo_bands, tables):
        added = jnp.dot(halo[:, a:b].astype(bf16), table[...], preferred_element_type=f32)
        for i in range(19):
            here[i, :, lo:hi] = state_ref[16 * i : 16 * i + 16, lo:hi] + added[16 * i : 16 * i + 16] + WEIGHT[i]

    lane = lax.broadcasted_iota(jnp.int32, (1, LANES), 1)
    y, z = lane // PITCH - HALO, lane % PITCH - HALO
    inside = (y >= 0) & (y < BS) & (z >= 0) & (z < BS)
    for t in range(STEPS):
        depth_in = 16 if t < 2 else 8
        depth_out = 16 if t < 1 else 8
        for i, (cx, cy, cz) in enumerate(VEL):
            value = here[i, 0:depth_in, :]
            shift = (cy * PITCH + cz) % LANES
            if shift:
                value = pltpu.roll(value, shift, 1)
            if cx:
                value = pltpu.roll(value, cx % depth_in, 0)
            there[i, 0:depth_out, :] = value[0:depth_out]
        total = there[0, 0:8, :]
        for i in range(1, 19):
            total = total + there[i, 0:8, :]
        seen[8 * t : 8 * t + 8, :] = jnp.where(inside, total - 1.0, 0.0)
        if t < STEPS - 1:

            def one(c, _):
                at = pl.ds(pl.multiple_of(c * 128, 128), 128)
                for i, value in enumerate(collide([there[i, 0:depth_out, at] for i in range(19)])):
                    here[i, 0:depth_out, at] = value
                return 0

            lax.fori_loop(0, LANES // 128, one, 0)
    for i in range(19):
        field_ref[8 * i : 8 * i + 8, :] = jnp.where(inside, there[i, 0:8, :], 0.0)

    rest_of = seen[...]
    read = jnp.zeros((8 * STEPS, 128), f32)
    for _ in range(3):
        piece = rest_of.astype(bf16)
        read = read + jnp.dot(piece, chosen_ref[...], preferred_element_type=f32)
        rest_of = rest_of - piece.astype(f32)
    before = spec_ref[256:257, :]
    layer = spec_ref[264:265, :]
    news = [[], []]
    for t in range(STEPS):
        value = jnp.zeros((1, 128), f32)
        for x in range(SLAB):
            row = 8 * t + OWN_ROW + x
            value = jnp.where(layer == x, read[row : row + 1], value)
        value = GAIN * value
        news[0].append(value.astype(bf16).astype(f32))
        news[1].append((value - before).astype(bf16).astype(f32))
        before = value
    for g in range(2):
        total = spec_ref[128 * g : 128 * g + 128, :]
        for t in range(STEPS):
            total = total + table_ref[:, t : t + 1] * news[g][t]
        out_ref[128 * g : 128 * g + 128, :] = total.astype(bf16)
    late[0:8, :] = geo_ref[...]
    late[8:16, :] = spec_ref[264:272, :]
    out_ref[256:272, :] = late[...].astype(bf16)


def field_kernel(bands, field_ref, *rest):
    own_refs, (out_ref,) = rest[: len(bands)], rest[len(bands) :]
    for (lo, hi, a, b), own_ref in zip(bands, own_refs):
        part = field_ref[:, a:b]
        coarse = part.astype(bf16)
        fine = (part - coarse.astype(f32)).astype(bf16)
        value = jnp.dot(coarse, own_ref[...], preferred_element_type=f32)
        value = value + jnp.dot(fine, own_ref[...], preferred_element_type=f32)
        for i in range(19):
            out_ref[0, i, :, lo:hi] = value[8 * i + OWN_ROW : 8 * i + OWN_ROW + 4]


def series(x, coefficients):
    value = coefficients[-1]
    for c in coefficients[-2::-1]:
        value = value * x + c
    return value


COSINE = [(-1.0) ** n / math.factorial(2 * n) for n in range(7)]
SINE = [(-1.0) ** n / math.factorial(2 * n + 1) for n in range(7)]
EARS = 32


def radiate_kernel(all_ref, listen_ref, out_ref, rows, spots, sums, goal):
    slot = lax.broadcasted_iota(jnp.int32, (128, 128), 0).astype(f32)
    base = jnp.zeros((1, 128), f32)
    for o in range(8):
        live = all_ref[o, 256:272, :].astype(f32)[9:10]
        goal[128 * o : 128 * o + 128, :] = jnp.where(slot < live, slot + base, -1.0)
        base = base + live
    everything = jnp.concatenate([all_ref[o] for o in range(8)], axis=1)
    used = jnp.max(base).astype(jnp.int32)
    for axis in range(3):
        spots[axis] = jnp.broadcast_to(listen_ref[axis : axis + 1, :], (128, 128)).T
    lane = lax.broadcasted_iota(jnp.int32, (1, 128), 1)
    lanes = lax.broadcasted_iota(jnp.int32, (EARS, 128), 1)
    shape = (EARS // 8, 8, 128)

    def panels(p, first, final):
        here = onehot(goal[...] == (lane + 128 * p).astype(f32))
        flat = jnp.dot(everything, here, preferred_element_type=f32)
        rows[...] = jnp.broadcast_to(flat[:, None, :], (272, 8, 128))

        def listeners(m, _):
            ears = pl.ds(pl.multiple_of(m * EARS, EARS), EARS)
            distance_sq = jnp.zeros(shape, f32)
            facing = jnp.zeros(shape, f32)
            for axis in range(3):
                offset = spots[axis, ears, :].reshape(shape) - rows[256 + axis]
                distance_sq = distance_sq + offset * offset
                facing = facing + rows[259 + axis] * offset
            distance = jnp.sqrt(distance_sq)
            far = facing / (4.0 * math.pi * SOUND * distance_sq)
            ratio = SOUND / distance
            angle = (2.0 * math.pi / SAMPLES) * (distance / SOUND)
            square = angle * angle
            cosine = series(square, COSINE)
            double = cosine + cosine
            c_before, s_before = far, jnp.zeros(shape, f32)
            c_now, s_now = far * cosine, far * (angle * series(square, SINE))
            result = jnp.zeros((EARS, 128), f32)
            for k in range(BINS):
                weight_real = rows[128 + k] + ratio * rows[k]
                weight_imag = rows[192 + k] + ratio * rows[64 + k]
                real = weight_real * c_now + weight_imag * s_now
                imag = weight_imag * c_now - weight_real * s_now
                for n, value in ((k, real), (BINS + k, imag)):
                    value = value.reshape(EARS, 128)
                    at = slice(128 * n, 128 * n + 128)
                    if first:
                        sums[ears, at] = value
                    elif not final:
                        sums[ears, at] += value
                    else:
                        whole = jnp.sum(sums[ears, at] + value, axis=1, keepdims=True)
                        result = jnp.where(lanes == n, whole, result)
                if k < BINS - 1:
                    c_now, c_before = double * c_now - c_before, c_now
                    s_now, s_before = double * s_now - s_before, s_now
            if final:
                out_ref[ears, :] = result
            return 0

        lax.fori_loop(0, 128 // EARS, listeners, 0)
        return 0

    tiles = jnp.maximum((used + 127) // 128, 2)
    panels(0, True, False)
    lax.fori_loop(1, tiles - 1, lambda p, _: panels(p, False, False), 0)
    panels(tiles - 1, False, True)


def call(kernel, outs, operands, scratch=(), megabytes=32, flops=0, fetch=False, store=False):
    vmem, anywhere = (pl.BlockSpec(memory_space=space) for space in (pltpu.VMEM, pl.ANY))
    block = anywhere if fetch else vmem
    return pl.pallas_call(
        kernel,
        out_shape=tuple(jax.ShapeDtypeStruct(s, d) for s, d in outs),
        in_specs=[block] * len(operands),
        out_specs=tuple(anywhere if store else vmem for _ in outs),
        scratch_shapes=[pltpu.VMEM(s, f32) if isinstance(s, tuple) else s for s in scratch],
        compiler_params=pltpu.CompilerParams(vmem_limit_bytes=megabytes * 2**20),
        cost_estimate=pl.CostEstimate(flops=flops, bytes_accessed=2**20, transcendentals=0),
    )(*operands)


def body(
    populations,
    block_faces,
    block_edges,
    probe_cell,
    history,
    panel_count,
    panel_owner,
    panel_pos,
    panel_normal,
    observers,
):
    own = own_table()
    around = halo_table()
    bands = [(lo, hi, *band(own, lo, hi)) for lo, hi in tiles_of(LANES, 256)]
    halo_bands = [(lo, hi, *band(around, lo, hi)) for lo, hi in tiles_of(LANES, 256)]
    back = own.T
    back_bands = [(lo, hi, *band(back, lo, hi)) for lo, hi in tiles_of(CELLS, 256)]

    def cut(table, ranges):
        return [jnp.asarray(table[a:b, lo:hi].astype(jnp.bfloat16)) for lo, hi, a, b in ranges]

    table = transform_table()
    shifted = np.concatenate([np.zeros((STEPS, 128), table.dtype), table[: SAMPLES - STEPS]]).T
    late = np.zeros((128, 128), np.float32)
    late[:, :STEPS] = table[SAMPLES - STEPS :].astype(np.float32).T
    operands = [
        populations,
        block_faces,
        block_edges,
        panel_count,
        panel_owner.reshape(1, 128),
        panel_pos,
        panel_normal,
        probe_cell.reshape(1, 128),
    ]
    results = [
        ((80, CELLS), f32),
        ((80, CELLS), bf16),
        ((64, 8, 128), bf16),
        ((160, 128), f32),
    ]
    collided, rounded, message, facts = call(
        pack_kernel,
        results,
        operands,
        scratch=[
            (pltpu.SMEM if 0 < n < 4 else pltpu.VMEM)(a.shape, a.dtype) for n, a in enumerate(operands)
        ]
        + [pltpu.VMEM(s, d) for s, d in results]
        + [(80, 640), (512, 128), pltpu.SemaphoreType.DMA((8,)), pltpu.SemaphoreType.DMA((4,))],
        megabytes=60,
        fetch=True,
        store=True,
    )
    ring = lax.axis_size("obs")
    up = [(i, (i + 1) % ring) for i in range(ring)]
    down = [(i, (i - 1) % ring) for i in range(ring)]

    def beside(value):
        return lax.ppermute(value, "obs", up), lax.ppermute(value, "obs", down)

    low, high = beside(rounded)
    spread = lax.all_to_all(message, "blk", 0, 0, tiled=True)
    sent, facts = call(
        forward_kernel,
        [((64, 8, 128), bf16), ((160, 128), f32)],
        [spread, facts],
        scratch=[(512, 128), (512, 128), (128, P_OWN)],
    )
    arrived = lax.all_to_all(sent, "blk", 0, 0, tiled=True)
    spec, newest_table, chosen, *tables = call(
        functools.partial(slots_kernel, halo_bands),
        [((272, 128), f32), ((128, 128), f32), ((LANES, 128), bf16)]
        + [((b - a, hi - lo), bf16) for lo, hi, a, b in halo_bands],
        [facts, history, jnp.asarray(shifted), jnp.asarray(late)],
        flops=10**8,
    )
    arrived, spec, newest_table, chosen, tables = lax.optimization_barrier(
        (arrived, spec, newest_table, chosen, tables)
    )
    arrived_low, arrived_high = beside(arrived)
    state, geometry = call(
        functools.partial(early_kernel, bands),
        [((304, LANES), f32), ((8, 128), f32)],
        [collided, low, high, arrived, facts],
        scratch=[(304, CELLS), (512, 128)],
        flops=10**8,
    )
    payload, field = call(
        functools.partial(flow_kernel, halo_bands),
        [((272, 128), bf16), ((152, LANES), f32)],
        [state, arrived, arrived_low, arrived_high, spec, newest_table, chosen, geometry, *tables],
        scratch=[(512, 128), (304, 640), (19, 16, LANES), (19, 16, LANES), (32, LANES), (16, 128)],
    )
    (populations_out,) = call(
        functools.partial(field_kernel, back_bands),
        [((1, 19, SLAB, CELLS), f32)],
        [field, *cut(back, back_bands)],
        flops=10**9,
    )
    gathered = lax.all_gather(payload, "obs", axis=0, tiled=False)
    (partial_value,) = call(
        radiate_kernel,
        [((128, 128), f32)],
        [gathered, observers],
        scratch=[(272, 8, 128), (3, 128, 128), (128, 16384), (1024, 128)],
        megabytes=20,
    )
    pieces = lax.all_to_all(partial_value.reshape(64, 256), "blk", 0, 0, tiled=True)
    summed = jnp.sum(pieces, axis=0)
    return (populations_out, summed.reshape(1, 2, 2 * BINS))


def solution(mesh):
    placed = (
        P("blk", None, "obs", None),
        P("blk", None),
        P("blk", None),
        P(("blk", "obs")),
        P(("blk", "obs"), None),
        P(("blk", "obs")),
        P(("blk", "obs")),
        P(None, ("blk", "obs")),
        P(None, ("blk", "obs")),
        P(None, "obs"),
    )
    return jax.shard_map(
        body,
        mesh=mesh,
        in_specs=placed,
        out_specs=(P("blk", None, "obs", None), P("obs", "blk", None)),
        check_vma=False,
    )
```
